32 devices in a mesh: ctx: 8 (over z, core), head: 4 (over y, x).
Axes of the slice: x: 2, y: 2, z: 4, core: 2. Of those that a mesh axis runs over, the one named last changes fastest.
Arguments:
- hidden: bfloat16 [4096, 4096], P('ctx'), may hold values from -6 to 6
- base_ids: int32 [4096], P('ctx'), may hold values from 0 to 4
- norm_gain: float32 [4096], replicated, may hold values from 0.1 to 1.9
- w_gate: bfloat16 [4096, 4096], P(None, 'head'), may hold values from -0.09375 to 0.09375
- w_value: bfloat16 [4096, 4096], P(None, 'head'), may hold values from -0.09375 to 0.09375
- w_bc: bfloat16 [4096, 256], replicated, may hold values from -0.09375 to 0.09375
- w_step: bfloat16 [4096, 64], P(None, 'head'), may hold values from -0.09375 to 0.09375
- conv_value: float32 [4, 4096], P(None, 'head'), may hold values from -3 to 3
- conv_bc: float32 [4, 256], replicated, may hold values from -3 to 3
- step_bias: float32 [64], P('head'), may hold values from -5.5 to -3.5
- decay_rate: float32 [64], P('head'), as said below
- skip_gain: float32 [64], P('head'), may hold values from 0.5 to 1.5
- out_gain: float32 [4096], P('head'), may hold values from 0.1 to 1.9
- w_out: bfloat16 [4096, 4096], P('head'), may hold values from -0.09375 to 0.09375
Outputs:
- mixed_out: bfloat16 [4096, 4096], P('ctx', 'head')
The draws below stay inside these ranges and needn't reach their ends.
Inputs may be any that keep to these rules, and one draw needn't show every extreme that they name: `base_ids`: 4 marks an unknown base N, 0 to 3 are A, C, G, T. `decay_rate`: positive rates.
All inputs are finite; a program needn't handle non-finite values.
Results may differ from the reference program's by a relative error of at most 0.0059.
Values may be sent and summed in bfloat16 or wider, within the bound.
A program may use at most 192 MiB of HBM per device.

```python
import jax
import jax.numpy as jnp
from jax import lax

D = 4096
HEADS = 64
HEAD_DIM = 64
STATE = 128
CONV_WIDTH = 4
BLOCK = 256
INNER = 4096
TOKENS = 4096


def draw_decay_rate(key, part):
    uniform_draw = jax.random.uniform(key, (HEADS,), jnp.float32)
    lowest = jnp.log(1.0 / TOKENS)
    highest = jnp.log(8.0)
    return jnp.exp(lowest + uniform_draw * (highest - lowest)).astype(jnp.float32)


def plant(array, own_key, smallest, high):
    dims = array.shape
    index_at = [jax.random.randint(jax.random.fold_in(own_key, axis), (), 0, dims[axis]) for axis in range(len(dims))]
    array = array.at[tuple(index_at)].set(smallest)
    longest = dims.index(max(dims))
    index_at[longest] = (index_at[longest] + 1) % dims[longest]
    return array.at[tuple(index_at)].set(high)


def levels(key, dims, cuts, smallest, largest):
    factor_of = 1.0
    for dim, shards_of in cuts:
        heights = jax.random.uniform(jax.random.fold_in(jax.random.fold_in(key, 6), dim), (shards_of,), jnp.float32, smallest / len(cuts), largest / len(cuts))
        factor_of = factor_of * jnp.repeat(jnp.exp(heights), dims[dim] // shards_of).reshape((-1,) + (1,) * (len(dims) - 1 - dim))
    return factor_of


def normal_values(rng, extent, spread, limit, cuts=(), held_as=jnp.bfloat16):
    loudness = levels(rng, extent, cuts, -0.22, 0.18) if cuts else 1.0
    drawn = jax.random.normal(rng, extent, jnp.float32) * spread * loudness
    return jnp.minimum(jnp.maximum(drawn, -limit), limit).astype(held_as)


def setup_inputs(seed: int = 0) -> dict:
    key_list = jax.random.split(jax.random.key(seed), 15)
    hidden = normal_values(key_list[0], (TOKENS, D), 1.0, 6.0, ((0, 8),))
    base_ids = plant(jax.random.randint(key_list[1], (TOKENS,), 0, 5), jax.random.fold_in(key_list[1], 1), 0, 4).astype(jnp.int32)
    norm_gain = jnp.clip(1.0 + 0.18 * jax.random.normal(key_list[2], (D,), jnp.float32), 0.1, 1.9)
    w_gate = normal_values(key_list[3], (D, INNER), D ** -0.5, 0.09375, ((1, 4),))
    w_value = normal_values(key_list[4], (D, INNER), D ** -0.5, 0.09375, ((1, 4),))
    w_bc = normal_values(key_list[5], (D, 2 * STATE), D ** -0.5, 0.09375)
    w_step = normal_values(key_list[6], (D, HEADS), D ** -0.5, 0.09375, ((1, 4),))
    conv_value = normal_values(key_list[7], (CONV_WIDTH, INNER), CONV_WIDTH ** -0.5, 3.0, ((1, 4),), jnp.float32)
    conv_bc = normal_values(key_list[8], (CONV_WIDTH, 2 * STATE), CONV_WIDTH ** -0.5, 3.0, (), jnp.float32)
    step_bias = jnp.clip(-5.5 + 2.0 * jax.random.uniform(key_list[9], (HEADS,), jnp.float32) ** levels(key_list[9], (HEADS,), ((0, 4),), -0.2, 0.2), -5.5, -3.5)
    decay_rate = draw_decay_rate(jax.random.fold_in(key_list[14], 71), 0)
    skip_gain = jnp.clip(0.5 + 1.0 * jax.random.uniform(key_list[11], (HEADS,), jnp.float32) ** levels(key_list[11], (HEADS,), ((0, 4),), -0.2, 0.2), 0.5, 1.5)
    out_gain = jnp.clip(1.0 + 0.18 * jax.random.normal(key_list[12], (INNER,), jnp.float32), 0.1, 1.9)
    w_out = normal_values(key_list[13], (INNER, D), INNER ** -0.5, 0.09375, ((0, 4),))
    return {"hidden": hidden, "base_ids": base_ids, "norm_gain": norm_gain, "w_gate": w_gate, "w_value": w_value, "w_bc": w_bc, "w_step": w_step, "conv_value": conv_value, "conv_bc": conv_bc, "step_bias": step_bias, "decay_rate": decay_rate, "skip_gain": skip_gain, "out_gain": out_gain, "w_out": w_out}


EPSILON = 1e-05
PRECISE = lax.Precision.HIGHEST

def convolve(padded, kernel, kernel_len):
    length = padded.shape[0] - 2 * (kernel_len - 1)
    reach = 2 * (kernel_len - 1)
    forward_sum = kernel[0] * padded[0:length]
    backward_sum = kernel[0] * padded[reach:reach + length]
    for offset in range(1, kernel_len):
        forward_sum = forward_sum + kernel[offset] * padded[offset:offset + length]
        backward_sum = backward_sum + kernel[offset] * padded[reach - offset:reach - offset + length]
    return (forward_sum, backward_sum)

def scan_blocks(values, inputs_b, inputs_c, steps, log_decay):
    block_total = TOKENS // BLOCK

    def blocked(source_array):
        return source_array.reshape((block_total, BLOCK) + source_array.shape[1:])
    causal = jnp.arange(BLOCK)[:, None] >= jnp.arange(BLOCK)[None, :]

    def advance(state_carry, block_item):
        value_rows, b_rows, c_rows, step_rows, decay_rows = block_item
        cumulative = jnp.cumsum(decay_rows, axis=0)
        scores = jnp.dot(c_rows, b_rows.T, precision=PRECISE)
        gaps = cumulative[:, None, :] - cumulative[None, :, :]
        weights = jnp.exp(jnp.where(causal[:, :, None], gaps, -jnp.inf)) * scores[:, :, None] * step_rows[None, :, :]
        within = jnp.einsum('tsh,shp->thp', weights, value_rows, precision=PRECISE)
        across = jnp.exp(cumulative)[:, :, None] * jnp.einsum('tn,hpn->thp', c_rows, state_carry, precision=PRECISE)
        tail_weight = jnp.exp(cumulative[-1:] - cumulative) * step_rows
        new_state = jnp.exp(cumulative[-1])[:, None, None] * state_carry + jnp.einsum('sh,sn,shp->hpn', tail_weight, b_rows, value_rows, precision=PRECISE)
        return (new_state, within + across)
    start_state = jnp.zeros((HEADS, HEAD_DIM, STATE), jnp.float32)
    final_state, outputs = lax.scan(advance, start_state, (blocked(values), blocked(inputs_b), blocked(inputs_c), blocked(steps), blocked(log_decay)))
    return outputs.reshape(TOKENS, HEADS, HEAD_DIM)

def mixer(hidden_rows, keep_mask, norm_gain, w_gate, w_value, w_bc, w_step, conv_value, conv_bc, step_bias, decay_rate, skip_gain, out_gain, w_out):
    inv_rms = lax.rsqrt(lax.optimization_barrier(jnp.mean(jnp.square(hidden_rows.astype(jnp.float32)), axis=-1)) + EPSILON)
    scaled = (hidden_rows * norm_gain).astype(jnp.bfloat16)

    def project(weight):
        return jnp.dot(scaled, weight, preferred_element_type=jnp.float32) * inv_rms[:, None]
    gate_in = project(w_gate)
    value_in = project(w_value)
    bc_in = project(w_bc)
    step_in = project(w_step)
    mixed_in = jnp.concatenate([value_in, bc_in], axis=-1)
    kernel = jnp.concatenate([conv_value, conv_bc], axis=-1)
    padded = jnp.pad(mixed_in, ((CONV_WIDTH - 1, CONV_WIDTH - 1), (0, 0)))
    forward_mix, backward_mix = convolve(padded, kernel, CONV_WIDTH)
    forward_mix = jax.nn.silu(forward_mix)
    backward_mix = jax.nn.silu(backward_mix)
    steps = jax.nn.softplus(step_in + step_bias)
    log_decay = -decay_rate * steps

    def split_lane(mixed_lane):
        values = (mixed_lane[:, :INNER] * keep_mask[:, None]).reshape(TOKENS, HEADS, HEAD_DIM)
        return (values, mixed_lane[:, INNER:INNER + STATE], mixed_lane[:, INNER + STATE:])
    fwd_values, fwd_b, fwd_c = split_lane(forward_mix)
    bwd_values, bwd_b, bwd_c = split_lane(backward_mix)
    forward_out = scan_blocks(fwd_values, fwd_b, fwd_c, steps, log_decay) + skip_gain[:, None] * fwd_values
    backward_out = scan_blocks(bwd_values[::-1], bwd_b[::-1], bwd_c[::-1], steps[::-1], log_decay[::-1])[::-1] + skip_gain[:, None] * bwd_values
    summed = forward_out + backward_out
    gated = summed * jax.nn.silu(gate_in).reshape(TOKENS, HEADS, HEAD_DIM)
    normed = (gated * lax.rsqrt(lax.optimization_barrier(jnp.mean(jnp.square(gated), axis=-1, keepdims=True)) + EPSILON) * out_gain.reshape(HEADS, HEAD_DIM)).astype(jnp.bfloat16)
    return jnp.dot(normed.reshape(TOKENS, INNER), w_out, preferred_element_type=jnp.float32)

def reference(hidden, base_ids, norm_gain, w_gate, w_value, w_bc, w_step, conv_value, conv_bc, step_bias, decay_rate, skip_gain, out_gain, w_out):
    keep_mask = (base_ids != 4).astype(jnp.float32)
    weights = (norm_gain, w_gate, w_value, w_bc, w_step, conv_value, conv_bc, step_bias, decay_rate, skip_gain, out_gain, w_out)
    branch_own = mixer(hidden, keep_mask, *weights)
    branch_other = mixer(hidden[::-1, ::-1], keep_mask[::-1], *weights)
    return (branch_own + branch_other[::-1, ::-1]).astype(jnp.bfloat16)
```

```python
import functools

import jax
import jax.numpy as jnp
from jax import lax
from jax.experimental import pallas as pl
from jax.experimental.pallas import tpu as pltpu
from jax.sharding import PartitionSpec as P

EPSILON = 1e-05
PRECISE = lax.Precision.HIGHEST
F32 = jnp.float32
BF16 = jnp.bfloat16
COLS = 256
ROWS = 128
HALO = 8
VMEM_LIMIT = 56 * 1024 * 1024


def params(dims):
    return pltpu.CompilerParams(
        vmem_limit_bytes=VMEM_LIMIT, dimension_semantics=("arbitrary",) * dims
    )


def anti_identity(size):
    row = lax.broadcasted_iota(jnp.int32, (size, size), 0)
    col = lax.broadcasted_iota(jnp.int32, (size, size), 1)
    return (row + col == size - 1).astype(F32).astype(BF16)


def matmul(a, b):
    return jnp.dot(a, b, preferred_element_type=F32)


def spread(per_head, width):
    heads = per_head.shape[1]
    high = per_head.astype(BF16)
    low = (per_head - high.astype(F32)).astype(BF16)
    row = lax.broadcasted_iota(jnp.int32, (heads, heads * width), 0)
    col = lax.broadcasted_iota(jnp.int32, (heads, heads * width), 1)
    pick = ((col >= row * width) & (col < (row + 1) * width)).astype(F32).astype(BF16)
    return matmul(high, pick) + matmul(low, pick)


def silu(x):
    return x * (1.0 / (1.0 + jnp.exp(-x)))


def prepare_kernel(own_ref, mirror_ref, gain_ref, scaled_ref, squares_ref):
    own = own_ref[...].astype(F32)
    gain = gain_ref[...]
    scaled_ref[0] = (own * gain).astype(BF16)
    flipped = matmul(mirror_ref[...], anti_identity(COLS))
    scaled_ref[1] = (flipped * gain).astype(BF16)

    @pl.when(pl.program_id(0) == 0)
    def _():
        squares_ref[...] = jnp.zeros_like(squares_ref)

    square = own * own
    squares_ref[...] += square[:, :128] + square[:, 128:]


def prepare(hidden, gain):
    length, depth = hidden.shape
    count = depth // COLS
    return pl.pallas_call(
        prepare_kernel,
        grid=(count,),
        in_specs=[
            pl.BlockSpec((length, COLS), lambda j: (0, j)),
            pl.BlockSpec((length, COLS), lambda j: (0, count - 1 - j)),
            pl.BlockSpec((1, COLS), lambda j: (0, j)),
        ],
        out_specs=[
            pl.BlockSpec((2, length, COLS), lambda j: (0, 0, j)),
            pl.BlockSpec((length, 128), lambda j: (0, 0)),
        ],
        out_shape=[
            jax.ShapeDtypeStruct((2, length, depth), BF16),
            jax.ShapeDtypeStruct((length, 128), F32),
        ],
        compiler_params=params(1),
        name="prepare",
    )(hidden, hidden, gain[None])


def convolve(out, ext, main_ref, before_ref, after_ref, taps_ref):
    length = main_ref.shape[1]
    ext[0:HALO] = before_ref[0]
    ext[HALO : HALO + length] = main_ref[0]
    ext[HALO + length :] = after_ref[0]
    taps = [taps_ref[k : k + 1, :] for k in range(4)]
    step = 64
    for start in range(0, length, step):
        rows = [ext[start + HALO - 3 + k : start + HALO - 3 + k + step] for k in range(7)]
        forward = taps[0] * rows[0]
        backward = taps[0] * rows[6]
        for k in range(1, 4):
            forward = forward + taps[k] * rows[k]
            backward = backward + taps[k] * rows[6 - k]
        out(start, step, silu(forward), silu(backward))


def mix_kernel(
    v_ref, bc_ref, before_v, before_bc, after_v, after_bc, taps_v, taps_bc, aux_ref, keep_ref,
    x_ref, bco_ref, bt_ref, s_ref, ext,
):
    c = pl.program_id(1)
    length = v_ref.shape[1]

    @pl.when(c == 0)
    def _():
        def out(start, step, forward, backward):
            bco_ref[0, 0, start : start + step] = forward.astype(BF16)
            bco_ref[0, 1, start : start + step] = backward.astype(BF16)

        convolve(out, ext, bc_ref, before_bc, after_bc, taps_bc)
        state = bt_ref.shape[2]
        for d in range(2):
            bt_ref[0, d] = bco_ref[0, d, :, :state].astype(F32).T.astype(BF16)

    @pl.when(c > 0)
    def _():
        def out(start, step, forward, backward):
            keep = keep_ref[start : start + step]
            x_ref[0, 0, start : start + step] = (forward * keep).astype(BF16)
            x_ref[0, 1, start : start + step] = (backward * keep).astype(BF16)

        convolve(out, ext, v_ref, before_v, after_v, taps_v)
        heads = aux_ref.shape[3] // 3
        aux = aux_ref[0, 0]
        steps = aux[:, 2 * heads :]
        for d in range(2):
            cum = aux[:, d * heads : (d + 1) * heads]
            total = cum[length - 1 :] if d == 0 else cum[:1]
            weight = spread(jnp.exp(total - cum) * steps, COLS // heads)
            s_ref[0, d] = matmul(bt_ref[0, d], (x_ref[0, d].astype(F32) * weight).astype(BF16))


def mix(value_in, bc_in, before, after, conv_value, conv_bc, aux, keep):
    _, length, inner = value_in.shape
    pair = bc_in.shape[2]
    state = pair // 2
    chunks = inner // COLS
    before_v, before_bc = before[..., :inner], before[..., inner:]
    after_v, after_bc = after[..., :inner], after[..., inner:]

    def at(c):
        return jnp.maximum(c - 1, 0)

    return pl.pallas_call(
        mix_kernel,
        grid=(2, chunks + 1),
        in_specs=[
            pl.BlockSpec((1, length, COLS), lambda b, c: (b, 0, at(c))),
            pl.BlockSpec((1, length, pair), lambda b, c: (b, 0, 0)),
            pl.BlockSpec((1, HALO, COLS), lambda b, c: (b, 0, at(c))),
            pl.BlockSpec((1, HALO, pair), lambda b, c: (b, 0, 0)),
            pl.BlockSpec((1, HALO, COLS), lambda b, c: (b, 0, at(c))),
            pl.BlockSpec((1, HALO, pair), lambda b, c: (b, 0, 0)),
            pl.BlockSpec((4, COLS), lambda b, c: (0, at(c))),
            pl.BlockSpec((4, pair), lambda b, c: (0, 0)),
            pl.BlockSpec((1, 1) + aux.shape[2:], lambda b, c: (b, at(c), 0, 0)),
            pl.BlockSpec((length, 1), lambda b, c: (0, 0)),
        ],
        out_specs=[
            pl.BlockSpec((1, 2, length, COLS), lambda b, c: (b, 0, 0, at(c))),
            pl.BlockSpec((1, 2, length, pair), lambda b, c: (b, 0, 0, 0)),
            pl.BlockSpec((1, 2, state, length), lambda b, c: (b, 0, 0, 0)),
            pl.BlockSpec((1, 2, state, COLS), lambda b, c: (b, 0, 0, at(c))),
        ],
        out_shape=[
            jax.ShapeDtypeStruct((2, 2, length, inner), BF16),
            jax.ShapeDtypeStruct((2, 2, length, pair), BF16),
            jax.ShapeDtypeStruct((2, 2, state, length), BF16),
            jax.ShapeDtypeStruct((2, 2, state, inner), F32),
        ],
        scratch_shapes=[pltpu.VMEM((length + 2 * HALO, COLS), F32)],
        compiler_params=params(2),
        cost_estimate=pl.CostEstimate(
            flops=2 * 4 * length * state * inner,
            bytes_accessed=14 * 2 * length * inner,
            transcendentals=4 * length * inner,
        ),
        name="mix",
    )(value_in, bc_in, before_v, before_bc, after_v, after_bc, conv_value, conv_bc, aux, keep)


def scan_kernel(x_ref, bc_ref, bt_ref, aux_ref, row_ref, skip_ref, y_ref):
    length = x_ref.shape[2]
    state = bt_ref.shape[2]
    heads = aux_ref.shape[3] // 3
    width = COLS // heads
    row = lax.broadcasted_iota(jnp.int32, (ROWS, ROWS), 0)
    col = lax.broadcasted_iota(jnp.int32, (ROWS, ROWS), 1)
    left = (lax.broadcasted_iota(jnp.int32, (1, 2 * width), 1) < width).astype(F32).astype(BF16)
    right = (1.0 - left.astype(F32)).astype(BF16)
    blocks = length // ROWS
    for d in range(2):
        carried = jnp.zeros((state, COLS), F32)
        reach = (row >= col) if d == 0 else (row <= col)
        order = range(blocks) if d == 0 else range(blocks - 1, -1, -1)
        for lap, i in enumerate(order):
            own = slice(i * ROWS, (i + 1) * ROWS)
            aux = aux_ref[0, 0, own]
            cum = aux[:, d * heads : (d + 1) * heads]
            steps = aux[:, 2 * heads :]
            x = x_ref[0, d, own].astype(F32)
            xd = x * spread(steps, width)
            xd16 = xd.astype(BF16)
            c_rows = bc_ref[0, d, own, state:]
            scores = lax.dot_general(
                c_rows, bc_ref[0, d, own, :state], (((1,), (1,)), ((), ())),
                preferred_element_type=F32,
            )
            scores = jnp.where(reach, scores, 0.0)
            parts = []
            for p in range(heads // 2):
                weights = []
                for h in (2 * p, 2 * p + 1):
                    line = row_ref[0, 0, d * heads + h : d * heads + h + 1, own]
                    gap = jnp.minimum(cum[:, h : h + 1] - line, 0.0)
                    weights.append((jnp.exp(gap) * scores).astype(BF16))
                both = xd16[:, 2 * p * width : 2 * (p + 1) * width]
                stacked = jnp.concatenate([both * left, both * right], axis=0)
                parts.append(matmul(jnp.concatenate(weights, axis=1), stacked))
            local = jnp.concatenate(parts, axis=1)
            if lap > 0:
                entry = (i * ROWS - 1) if d == 0 else (i + 1) * ROWS
                base = aux_ref[0, 0, entry : entry + 1, d * heads : (d + 1) * heads]
                local = local + spread(jnp.exp(cum - base), width) * matmul(
                    c_rows, carried.astype(BF16)
                )
            else:
                base = jnp.zeros((1, heads), F32)
            local = local + skip_ref[...] * x
            if d == 0:
                y_ref[0, own] = local
            else:
                y_ref[0, own] += local
            if lap < blocks - 1:
                last = cum[ROWS - 1 :] if d == 0 else cum[:1]
                tail = spread(jnp.exp(last - cum), width)
                fresh = matmul(bt_ref[0, d, :, own], (xd * tail).astype(BF16))
                if lap > 0:
                    decay = spread(jnp.broadcast_to(jnp.exp(last - base), (8, heads)), width)
                    carried = decay[:1] * carried + fresh
                else:
                    carried = fresh


def scan_local(x, bc, bt, aux, rows, skip):
    _, _, length, inner = x.shape
    pair = bc.shape[3]
    state = pair // 2
    chunks = inner // COLS
    return pl.pallas_call(
        scan_kernel,
        grid=(2, chunks),
        in_specs=[
            pl.BlockSpec((1, 2, length, COLS), lambda b, c: (b, 0, 0, c)),
            pl.BlockSpec((1, 2, length, pair), lambda b, c: (b, 0, 0, 0)),
            pl.BlockSpec((1, 2, state, length), lambda b, c: (b, 0, 0, 0)),
            pl.BlockSpec((1, 1) + aux.shape[2:], lambda b, c: (b, c, 0, 0)),
            pl.BlockSpec((1, 1) + rows.shape[2:], lambda b, c: (b, c, 0, 0)),
            pl.BlockSpec((1, COLS), lambda b, c: (0, c)),
        ],
        out_specs=pl.BlockSpec((1, length, COLS), lambda b, c: (b, 0, c)),
        out_shape=jax.ShapeDtypeStruct((2, length, inner), F32),
        compiler_params=params(2),
        cost_estimate=pl.CostEstimate(
            flops=2 * 64 * length * ROWS * inner,
            bytes_accessed=20 * length * inner,
            transcendentals=0,
        ),
        name="scan_local",
    )(x, bc, bt, aux, rows, skip)


def finish_kernel(y_ref, bc_ref, s_ref, aux_ref, gate_ref, gain_ref, out_ref):
    state = s_ref.shape[2]
    heads = aux_ref.shape[3] // 3
    width = COLS // heads
    row = lax.broadcasted_iota(jnp.int32, (COLS, COLS), 0)
    col = lax.broadcasted_iota(jnp.int32, (COLS, COLS), 1)
    same = None
    for h in range(heads):
        low, high = h * width, (h + 1) * width
        square = (row >= low) & (row < high) & (col >= low) & (col < high)
        same = square if same is None else same | square
    same = same.astype(F32).astype(BF16)
    length = y_ref.shape[1]
    for start in range(0, length, ROWS):
        own = slice(start, start + ROWS)
        aux = aux_ref[0, 0, own]
        y = y_ref[0, own]
        for d in range(2):
            grown = spread(jnp.exp(aux[:, d * heads : (d + 1) * heads]), width)
            y = y + grown * matmul(bc_ref[0, d, own, state:], s_ref[0, d])
        gated = y * silu(gate_ref[0, own])
        mean = matmul((gated * gated).astype(BF16), same) * (1.0 / width)
        out_ref[0, own] = (gated * lax.rsqrt(mean + EPSILON) * gain_ref[...]).astype(BF16)


def finish(y, bc, entering, aux, gate_in, gain):
    _, length, inner = y.shape
    pair = bc.shape[3]
    chunks = inner // COLS
    return pl.pallas_call(
        finish_kernel,
        grid=(2, chunks),
        in_specs=[
            pl.BlockSpec((1, length, COLS), lambda b, c: (b, 0, c)),
            pl.BlockSpec((1, 2, length, pair), lambda b, c: (b, 0, 0, 0)),
            pl.BlockSpec((1, 2, pair // 2, COLS), lambda b, c: (b, 0, 0, c)),
            pl.BlockSpec((1, 1) + aux.shape[2:], lambda b, c: (b, c, 0, 0)),
            pl.BlockSpec((1, length, COLS), lambda b, c: (b, 0, c)),
            pl.BlockSpec((1, COLS), lambda b, c: (0, c)),
        ],
        out_specs=pl.BlockSpec((1, length, COLS), lambda b, c: (b, 0, c)),
        out_shape=jax.ShapeDtypeStruct((2, length, inner), BF16),
        compiler_params=params(2),
        name="finish",
    )(y, bc, entering, aux, gate_in, gain)


def project_out_kernel(normed_ref, own_ref, mirror_ref, out_ref):
    flipped = matmul(mirror_ref[...], anti_identity(COLS)).astype(BF16)
    out_ref[...] = (
        matmul(normed_ref[0], own_ref[...]) + matmul(normed_ref[1], flipped)
    ).astype(BF16)


def project_out(normed, w_out):
    _, length, inner = normed.shape
    depth = w_out.shape[1]
    count = depth // COLS
    return pl.pallas_call(
        project_out_kernel,
        grid=(count,),
        in_specs=[
            pl.BlockSpec((2, length, inner), lambda j: (0, 0, 0)),
            pl.BlockSpec((inner, COLS), lambda j: (0, j)),
            pl.BlockSpec((inner, COLS), lambda j: (0, count - 1 - j)),
        ],
        out_specs=pl.BlockSpec((length, COLS), lambda j: (0, j)),
        out_shape=jax.ShapeDtypeStruct((length, depth), BF16),
        compiler_params=params(1),
        name="project_out",
    )(normed, w_out, w_out)


def enter_states(local, log_total, width):
    size = lax.axis_size("ctx")
    odd = lax.axis_index("ctx") % 2 == 1
    swap = [(i, i ^ 1) for i in range(size)]
    ahead = [(i, i + 2) for i in range(1, size - 2, 2)] + [(i, i - 2) for i in range(2, size, 2)]
    decay = jnp.repeat(jnp.exp(log_total), width, axis=-1)[:, None, :]
    other_decay = jnp.repeat(
        jnp.exp(lax.ppermute(log_total, "ctx", swap)), width, axis=-1
    )[:, None, :]
    chip_decay = decay * other_decay
    forward, backward = local[:, 0], local[:, 1]
    received = lax.ppermute(jnp.where(odd, backward, forward).astype(BF16), "ctx", swap).astype(F32)
    chip = decay * received + jnp.where(odd, forward, backward)
    entering = lax.ppermute(chip.astype(BF16), "ctx", ahead)
    for _ in range(size // 2 - 2):
        entering = lax.ppermute(
            (chip + chip_decay * entering.astype(F32)).astype(BF16), "ctx", ahead
        )
    crossed = lax.ppermute(entering, "ctx", swap)
    own = (other_decay * entering.astype(F32) + received).astype(BF16)
    return jnp.stack([jnp.where(odd, own, crossed), jnp.where(odd, crossed, own)], axis=1)


def shards(
    hidden, base_ids, norm_gain, w_gate, w_value, w_bc, w_step, conv_value, conv_bc,
    step_bias, decay_rate, skip_gain, out_gain, w_out,
):
    keep = (base_ids != 4).astype(F32)[:, None]
    length, depth = hidden.shape
    inner = w_gate.shape[1]
    heads = w_step.shape[1]
    width = inner // heads
    chunks = inner // COLS
    per = COLS // width
    scaled, squares = prepare(hidden, norm_gain)
    inv_rms = lax.rsqrt(jnp.sum(squares, axis=-1) / depth + EPSILON)[:, None]

    def project(weight):
        return (
            jnp.einsum("btd,dk->btk", scaled, weight, preferred_element_type=F32) * inv_rms
        )

    bc_in = project(w_bc)
    step_in = project(w_step)
    value_in = project(w_value)
    size = lax.axis_size("ctx")
    up = [(i, i + 1) for i in range(size - 1)]
    down = [(i + 1, i) for i in range(size - 1)]
    tail = jnp.concatenate([value_in[:, length - HALO :], bc_in[:, length - HALO :]], axis=-1)
    head = jnp.concatenate([value_in[:, :HALO], bc_in[:, :HALO]], axis=-1)
    before = lax.ppermute(tail, "ctx", up)
    after = lax.ppermute(head, "ctx", down)
    gate_in = project(w_gate)

    steps = jax.nn.softplus(step_in + step_bias)
    log_decay = -decay_rate * steps
    lower = jnp.tril(jnp.ones((length, length), F32))
    triangles = jnp.stack([lower, lower.T])
    cum = jnp.einsum("dts,bsh->bdth", triangles, log_decay, precision=PRECISE)
    log_total = cum[:, 0, -1]
    packed = jnp.concatenate([cum, steps[:, None]], axis=1)
    packed = packed.reshape(2, 3, length, chunks, per)
    aux = packed.transpose(0, 3, 2, 1, 4).reshape(2, chunks, length, 3 * per)
    rows = packed[:, :2].transpose(0, 3, 1, 4, 2).reshape(2, chunks, 2 * per, length)

    x, bc, bt, local = mix(value_in, bc_in, before, after, conv_value, conv_bc, aux, keep)
    entering = enter_states(local, log_total, width)
    y = scan_local(x, bc, bt, aux, rows, jnp.repeat(skip_gain, width)[None])
    normed = finish(y, bc, entering, aux, gate_in, out_gain[None])
    term = project_out(normed, w_out)
    return lax.psum_scatter(term, "head", scatter_dimension=1, tiled=True)


def solution(mesh):
    return jax.shard_map(
        shards,
        mesh=mesh,
        in_specs=(
            P("ctx", None),
            P("ctx"),
            P(),
            P(None, "head"),
            P(None, "head"),
            P(),
            P(None, "head"),
            P(None, "head"),
            P(),
            P("head"),
            P("head"),
            P("head"),
            P("head"),
            P("head", None),
        ),
        out_specs=P("ctx", "head"),
        check_vma=False,
    )
```

```python
import functools

import jax
import jax.numpy as jnp
from jax import lax
from jax.experimental import pallas as pl
from jax.experimental.pallas import tpu as pltpu
from jax.sharding import PartitionSpec as P

EPSILON = 1e-05
PRECISE = lax.Precision.HIGHEST
F32 = jnp.float32
BF16 = jnp.bfloat16
COLS = 256
ROWS = 128
HALO = 8
VMEM_LIMIT = 56 * 1024 * 1024


def params(dims):
    return pltpu.CompilerParams(
        vmem_limit_bytes=VMEM_LIMIT, dimension_semantics=("arbitrary",) * dims
    )


def anti_identity(size):
    row = lax.broadcasted_iota(jnp.int32, (size, size), 0)
    col = lax.broadcasted_iota(jnp.int32, (size, size), 1)
    return (row + col == size - 1).astype(F32).astype(BF16)


def matmul(a, b):
    return jnp.dot(a, b, preferred_element_type=F32)


def spread(per_head, width):
    heads = per_head.shape[1]
    high = per_head.astype(BF16)
    low = (per_head - high.astype(F32)).astype(BF16)
    row = lax.broadcasted_iota(jnp.int32, (heads, heads * width), 0)
    col = lax.broadcasted_iota(jnp.int32, (heads, heads * width), 1)
    pick = ((col >= row * width) & (col < (row + 1) * width)).astype(F32).astype(BF16)
    return matmul(high, pick) + matmul(low, pick)


def silu(x):
    return x * (1.0 / (1.0 + jnp.exp(-x)))


def prepare_kernel(own_ref, mirror_ref, gain_ref, scaled_ref, squares_ref):
    own = own_ref[...].astype(F32)
    gain = gain_ref[...]
    scaled_ref[0] = (own * gain).astype(BF16)
    flipped = matmul(mirror_ref[...], anti_identity(COLS))
    scaled_ref[1] = (flipped * gain).astype(BF16)

    @pl.when(pl.program_id(0) == 0)
    def _():
        squares_ref[...] = jnp.zeros_like(squares_ref)

    square = own * own
    squares_ref[...] += square[:, :128] + square[:, 128:]


def prepare(hidden, gain):
    length, depth = hidden.shape
    count = depth // COLS
    return pl.pallas_call(
        prepare_kernel,
        grid=(count,),
        in_specs=[
            pl.BlockSpec((length, COLS), lambda j: (0, j)),
            pl.BlockSpec((length, COLS), lambda j: (0, count - 1 - j)),
            pl.BlockSpec((1, COLS), lambda j: (0, j)),
        ],
        out_specs=[
            pl.BlockSpec((2, length, COLS), lambda j: (0, 0, j)),
            pl.BlockSpec((length, 128), lambda j: (0, 0)),
        ],
        out_shape=[
            jax.ShapeDtypeStruct((2, length, depth), BF16),
            jax.ShapeDtypeStruct((length, 128), F32),
        ],
        compiler_params=params(1),
        name="prepare",
    )(hidden, hidden, gain[None])


def convolve(out, ext, main_ref, before_ref, after_ref, taps_ref):
    length = main_ref.shape[1]
    ext[0:HALO] = before_ref[0]
    ext[HALO : HALO + length] = main_ref[0]
    ext[HALO + length :] = after_ref[0]
    taps = [taps_ref[k : k + 1, :] for k in range(4)]
    step = 64
    for start in range(0, length, step):
        rows = [ext[start + HALO - 3 + k : start + HALO - 3 + k + step] for k in range(7)]
        forward = taps[0] * rows[0]
        backward = taps[0] * rows[6]
        for k in range(1, 4):
            forward = forward + taps[k] * rows[k]
            backward = backward + taps[k] * rows[6 - k]
        out(start, step, silu(forward), silu(backward))


def mix_kernel(
    v_ref, bc_ref, before_v, before_bc, after_v, after_bc, taps_v, taps_bc, aux_ref, keep_ref,
    x_ref, bco_ref, bt_ref, s_ref, ext,
):
    c = pl.program_id(1)
    length = v_ref.shape[1]

    @pl.when(c == 0)
    def _():
        def out(start, step, forward, backward):
            bco_ref[0, 0, start : start + step] = forward.astype(BF16)
            bco_ref[0, 1, start : start + step] = backward.astype(BF16)

        convolve(out, ext, bc_ref, before_bc, after_bc, taps_bc)
        state = bt_ref.shape[2]
        for d in range(2):
            bt_ref[0, d] = bco_ref[0, d, :, :state].astype(F32).T.astype(BF16)

    @pl.when(c > 0)
    def _():
        def out(start, step, forward, backward):
            keep = keep_ref[start : start + step]
            x_ref[0, 0, start : start + step] = (forward * keep).astype(BF16)
            x_ref[0, 1, start : start + step] = (backward * keep).astype(BF16)

        convolve(out, ext, v_ref, before_v, after_v, taps_v)
        heads = aux_ref.shape[3] // 3
        aux = aux_ref[0, 0]
        steps = aux[:, 2 * heads :]
        for d in range(2):
            cum = aux[:, d * heads : (d + 1) * heads]
            total = cum[length - 1 :] if d == 0 else cum[:1]
            weight = spread(jnp.exp(total - cum) * steps, COLS // heads)
            s_ref[0, d] = matmul(bt_ref[0, d], (x_ref[0, d].astype(F32) * weight).astype(BF16))


def mix(value_in, bc_in, before, after, conv_value, conv_bc, aux, keep):
    _, length, inner = value_in.shape
    pair = bc_in.shape[2]
    state = pair // 2
    chunks = inner // COLS
    before_v, before_bc = before[..., :inner], before[..., inner:]
    after_v, after_bc = after[..., :inner], after[..., inner:]

    def at(c):
        return jnp.maximum(c - 1, 0)

    return pl.pallas_call(
        mix_kernel,
        grid=(2, chunks + 1),
        in_specs=[
            pl.BlockSpec((1, length, COLS), lambda b, c: (b, 0, at(c))),
            pl.BlockSpec((1, length, pair), lambda b, c: (b, 0, 0)),
            pl.BlockSpec((1, HALO, COLS), lambda b, c: (b, 0, at(c))),
            pl.BlockSpec((1, HALO, pair), lambda b, c: (b, 0, 0)),
            pl.BlockSpec((1, HALO, COLS), lambda b, c: (b, 0, at(c))),
            pl.BlockSpec((1, HALO, pair), lambda b, c: (b, 0, 0)),
            pl.BlockSpec((4, COLS), lambda b, c: (0, at(c))),
            pl.BlockSpec((4, pair), lambda b, c: (0, 0)),
            pl.BlockSpec((1, 1) + aux.shape[2:], lambda b, c: (b, at(c), 0, 0)),
            pl.BlockSpec((length, 1), lambda b, c: (0, 0)),
        ],
        out_specs=[
            pl.BlockSpec((1, 2, length, COLS), lambda b, c: (b, 0, 0, at(c))),
            pl.BlockSpec((1, 2, length, pair), lambda b, c: (b, 0, 0, 0)),
            pl.BlockSpec((1, 2, state, length), lambda b, c: (b, 0, 0, 0)),
            pl.BlockSpec((1, 2, state, COLS), lambda b, c: (b, 0, 0, at(c))),
        ],
        out_shape=[
            jax.ShapeDtypeStruct((2, 2, length, inner), BF16),
            jax.ShapeDtypeStruct((2, 2, length, pair), BF16),
            jax.ShapeDtypeStruct((2, 2, state, length), BF16),
            jax.ShapeDtypeStruct((2, 2, state, inner), F32),
        ],
        scratch_shapes=[pltpu.VMEM((length + 2 * HALO, COLS), F32)],
        compiler_params=params(2),
        cost_estimate=pl.CostEstimate(
            flops=2 * 4 * length * state * inner,
            bytes_accessed=14 * 2 * length * inner,
            transcendentals=4 * length * inner,
        ),
        name="mix",
    )(value_in, bc_in, before_v, before_bc, after_v, after_bc, conv_value, conv_bc, aux, keep)


def chain(size, last, local_ref, total_ref, ent_ref, swapped, decay_other, chip, kept,
          hop_out, hop_in, crossed, send_sems, recv_sems):
    me = lax.axis_index("ctx")
    odd = lax.rem(me, 2)
    hops = size // 2 - 1
    ahead = me + 4 * odd - 2
    behind = me - 4 * odd + 2
    has_ahead = (ahead >= 0) & (ahead < size)
    has_behind = (behind >= 0) & (behind < size)
    partner = me + 1 - 2 * odd

    def remote(source, target, index, device):
        return pltpu.make_async_remote_copy(
            src_ref=source,
            dst_ref=target,
            send_sem=send_sems.at[index],
            recv_sem=recv_sems.at[index],
            device_id={"ctx": device},
            device_id_type=pl.DeviceIdType.MESH,
        )

    swap_copy = remote(kept, swapped, 0, partner)
    decay_copy = remote(total_ref, decay_other, 1, partner)
    cross_copy = remote(kept, crossed, 2, partner)
    hop_copies = [remote(hop_out.at[k], hop_in.at[k], 3 + k, ahead) for k in range(hops)]

    def greet():
        barrier = pltpu.get_barrier_semaphore()

        def signal(device):
            pl.semaphore_signal(
                barrier, inc=1, device_id={"ctx": device}, device_id_type=pl.DeviceIdType.MESH
            )

        signal(partner)
        pl.when(has_ahead)(lambda: signal(ahead))
        pl.when(has_behind)(lambda: signal(behind))
        pl.semaphore_wait(
            barrier, 1 + has_ahead.astype(jnp.int32) + has_behind.astype(jnp.int32)
        )

    def first():
        greet()
        for b in range(2):
            kept[b] = jnp.where(odd == 1, local_ref[b, 1], local_ref[b, 0]).astype(BF16)
        swap_copy.start()
        decay_copy.start()

    def second():
        swap_copy.wait()
        decay_copy.wait()
        for b in range(2):
            mine = jnp.where(odd == 1, local_ref[b, 0], local_ref[b, 1])
            decay = jnp.exp(total_ref[b, :1])
            chip[b] = decay * swapped[b].astype(F32) + mine
            hop_out[0, b] = chip[b].astype(BF16)
        pl.when(has_ahead)(lambda: hop_copies[0].start())

    def entered(k, b):
        return jnp.where(has_behind, hop_in[k, b].astype(F32), 0.0)

    def hop(k):
        def stage():
            pl.when(has_behind)(lambda: hop_copies[k - 1].wait_recv())
            for b in range(2):
                decay = jnp.exp(total_ref[b, :1] + decay_other[b, :1])
                hop_out[k, b] = (chip[b] + decay * entered(k - 1, b)).astype(BF16)
            pl.when(has_ahead)(lambda: hop_copies[k].start())

        return stage

    def cross():
        pl.when(has_behind)(lambda: hop_copies[hops - 1].wait_recv())
        for b in range(2):
            kept[b] = entered(hops - 1, b).astype(BF16)
        cross_copy.start()

    def end():
        cross_copy.wait()
        for b in range(2):
            own = jnp.exp(decay_other[b, :1]) * kept[b].astype(F32) + swapped[b].astype(F32)
            other = crossed[b].astype(F32)
            ent_ref[b, 0] = jnp.where(odd == 1, own, other).astype(BF16)
            ent_ref[b, 1] = jnp.where(odd == 1, other, own).astype(BF16)
        for k in range(hops):
            pl.when(has_ahead)(lambda k=k: hop_copies[k].wait_send())

    stages = [first, second] + [hop(k) for k in range(1, hops)] + [cross]
    return [(min(last, (7 * i) // 5), stage) for i, stage in enumerate(stages)], end


def scan_kernel(size, x_ref, bc_ref, bt_ref, aux_ref, row_ref, skip_ref, local_ref, total_ref,
                y_ref, ent_ref, *scratch):
    step = pl.program_id(0) * pl.num_programs(1) + pl.program_id(1)
    last_step = 2 * (local_ref.shape[3] // COLS) - 1
    stages, end = chain(size, last_step, local_ref, total_ref, ent_ref, *scratch)
    for at, stage in stages:
        pl.when(step == at)(stage)
    length = x_ref.shape[2]
    state = bt_ref.shape[2]
    heads = aux_ref.shape[3] // 3
    width = COLS // heads
    row = lax.broadcasted_iota(jnp.int32, (ROWS, ROWS), 0)
    col = lax.broadcasted_iota(jnp.int32, (ROWS, ROWS), 1)
    left = (lax.broadcasted_iota(jnp.int32, (1, 2 * width), 1) < width).astype(F32).astype(BF16)
    right = (1.0 - left.astype(F32)).astype(BF16)
    blocks = length // ROWS
    for d in range(2):
        carried = jnp.zeros((state, COLS), F32)
        reach = (row >= col) if d == 0 else (row <= col)
        order = range(blocks) if d == 0 else range(blocks - 1, -1, -1)
        for lap, i in enumerate(order):
            own = slice(i * ROWS, (i + 1) * ROWS)
            aux = aux_ref[0, 0, own]
            cum = aux[:, d * heads : (d + 1) * heads]
            steps = aux[:, 2 * heads :]
            x = x_ref[0, d, own].astype(F32)
            xd = x * spread(steps, width)
            xd16 = xd.astype(BF16)
            c_rows = bc_ref[0, d, own, state:]
            scores = lax.dot_general(
                c_rows, bc_ref[0, d, own, :state], (((1,), (1,)), ((), ())),
                preferred_element_type=F32,
            )
            scores = jnp.where(reach, scores, 0.0)
            parts = []
            for p in range(heads // 2):
                weights = []
                for h in (2 * p, 2 * p + 1):
                    line = row_ref[0, 0, d * heads + h : d * heads + h + 1, own]
                    gap = jnp.minimum(cum[:, h : h + 1] - line, 0.0)
                    weights.append((jnp.exp(gap) * scores).astype(BF16))
                both = xd16[:, 2 * p * width : 2 * (p + 1) * width]
                stacked = jnp.concatenate([both * left, both * right], axis=0)
                parts.append(matmul(jnp.concatenate(weights, axis=1), stacked))
            local = jnp.concatenate(parts, axis=1)
            if lap > 0:
                entry = (i * ROWS - 1) if d == 0 else (i + 1) * ROWS
                base = aux_ref[0, 0, entry : entry + 1, d * heads : (d + 1) * heads]
                local = local + spread(jnp.exp(cum - base), width) * matmul(
                    c_rows, carried.astype(BF16)
                )
            else:
                base = jnp.zeros((1, heads), F32)
            local = local + skip_ref[...] * x
            if d == 0:
                y_ref[0, own] = local
            else:
                y_ref[0, own] += local
            if lap < blocks - 1:
                last = cum[ROWS - 1 :] if d == 0 else cum[:1]
                tail = spread(jnp.exp(last - cum), width)
                fresh = matmul(bt_ref[0, d, :, own], (xd * tail).astype(BF16))
                if lap > 0:
                    decay = spread(jnp.broadcast_to(jnp.exp(last - base), (8, heads)), width)
                    carried = decay[:1] * carried + fresh
                else:
                    carried = fresh
    pl.when(step == last_step)(end)


def scan_local(x, bc, bt, aux, rows, skip, local, total):
    size = lax.axis_size("ctx")
    hops = size // 2 - 1
    wide = local.shape[2:]
    _, _, length, inner = x.shape
    pair = bc.shape[3]
    state = pair // 2
    chunks = inner // COLS
    return pl.pallas_call(
        functools.partial(scan_kernel, size),
        grid=(2, chunks),
        in_specs=[
            pl.BlockSpec((1, 2, length, COLS), lambda b, c: (b, 0, 0, c)),
            pl.BlockSpec((1, 2, length, pair), lambda b, c: (b, 0, 0, 0)),
            pl.BlockSpec((1, 2, state, length), lambda b, c: (b, 0, 0, 0)),
            pl.BlockSpec((1, 1) + aux.shape[2:], lambda b, c: (b, c, 0, 0)),
            pl.BlockSpec((1, 1) + rows.shape[2:], lambda b, c: (b, c, 0, 0)),
            pl.BlockSpec((1, COLS), lambda b, c: (0, c)),
            pl.BlockSpec(local.shape, lambda b, c: (0, 0, 0, 0)),
            pl.BlockSpec(total.shape, lambda b, c: (0, 0, 0)),
        ],
        out_specs=[
            pl.BlockSpec((1, length, COLS), lambda b, c: (b, 0, c)),
            pl.BlockSpec(local.shape, lambda b, c: (0, 0, 0, 0)),
        ],
        out_shape=[
            jax.ShapeDtypeStruct((2, length, inner), F32),
            jax.ShapeDtypeStruct(local.shape, BF16),
        ],
        scratch_shapes=[
            pltpu.VMEM((2,) + wide, BF16),
            pltpu.VMEM(total.shape, F32),
            pltpu.VMEM((2,) + wide, F32),
            pltpu.VMEM((2,) + wide, BF16),
            pltpu.VMEM((hops, 2) + wide, BF16),
            pltpu.VMEM((hops, 2) + wide, BF16),
            pltpu.VMEM((2,) + wide, BF16),
            pltpu.SemaphoreType.DMA((3 + hops,)),
            pltpu.SemaphoreType.DMA((3 + hops,)),
        ],
        compiler_params=pltpu.CompilerParams(
            vmem_limit_bytes=VMEM_LIMIT,
            dimension_semantics=("arbitrary",) * 2,
            collective_id=1,
            has_side_effects=True,
        ),
        cost_estimate=pl.CostEstimate(
            flops=2 * 64 * length * ROWS * inner,
            bytes_accessed=20 * length * inner,
            transcendentals=0,
        ),
        name="scan_local",
    )(x, bc, bt, aux, rows, skip, local, total)


def finish_kernel(y_ref, bc_ref, s_ref, aux_ref, gate_ref, gain_ref, out_ref):
    state = s_ref.shape[2]
    heads = aux_ref.shape[3] // 3
    width = COLS // heads
    row = lax.broadcasted_iota(jnp.int32, (COLS, COLS), 0)
    col = lax.broadcasted_iota(jnp.int32, (COLS, COLS), 1)
    same = None
    for h in range(heads):
        low, high = h * width, (h + 1) * width
        square = (row >= low) & (row < high) & (col >= low) & (col < high)
        same = square if same is None else same | square
    same = same.astype(F32).astype(BF16)
    length = y_ref.shape[1]
    for start in range(0, length, ROWS):
        own = slice(start, start + ROWS)
        aux = aux_ref[0, 0, own]
        y = y_ref[0, own]
        for d in range(2):
            grown = spread(jnp.exp(aux[:, d * heads : (d + 1) * heads]), width)
            y = y + grown * matmul(bc_ref[0, d, own, state:], s_ref[0, d])
        gated = y * silu(gate_ref[0, own])
        mean = matmul((gated * gated).astype(BF16), same) * (1.0 / width)
        out_ref[0, own] = (gated * lax.rsqrt(mean + EPSILON) * gain_ref[...]).astype(BF16)


def finish(y, bc, entering, aux, gate_in, gain):
    _, length, inner = y.shape
    pair = bc.shape[3]
    chunks = inner // COLS
    return pl.pallas_call(
        finish_kernel,
        grid=(2, chunks),
        in_specs=[
            pl.BlockSpec((1, length, COLS), lambda b, c: (b, 0, c)),
            pl.BlockSpec((1, 2, length, pair), lambda b, c: (b, 0, 0, 0)),
            pl.BlockSpec((1, 2, pair // 2, COLS), lambda b, c: (b, 0, 0, c)),
            pl.BlockSpec((1, 1) + aux.shape[2:], lambda b, c: (b, c, 0, 0)),
            pl.BlockSpec((1, length, COLS), lambda b, c: (b, 0, c)),
            pl.BlockSpec((1, COLS), lambda b, c: (0, c)),
        ],
        out_specs=pl.BlockSpec((1, length, COLS), lambda b, c: (b, 0, c)),
        out_shape=jax.ShapeDtypeStruct((2, length, inner), BF16),
        compiler_params=params(2),
        name="finish",
    )(y, bc, entering, aux, gate_in, gain)


def project_out_kernel(
    count, normed_ref, w_ref, out_ref, held, sending, landed, send_sems, recv_sems
):
    me = lax.axis_index("head")
    bits = count.bit_length() - 1
    inner, depth = w_ref.shape
    half = depth // count // 2
    tile = min(half, COLS)
    orders = (list(range(bits)), list(range(bits))[::-1])

    barrier = pltpu.get_barrier_semaphore()
    for bit in range(bits):
        pl.semaphore_signal(
            barrier, inc=1, device_id={"head": me ^ (1 << bit)},
            device_id_type=pl.DeviceIdType.MESH,
        )
    pl.semaphore_wait(barrier, bits)

    def phase_of(side, mask):
        return next(p for p, bit in enumerate(orders[side]) if mask >> bit & 1)

    def copy_of(side, mask):
        slot = side * (count - 1) + mask - 1
        partner = me ^ (1 << orders[side][phase_of(side, mask)])
        return pltpu.make_async_remote_copy(
            src_ref=sending.at[slot],
            dst_ref=landed.at[slot],
            send_sem=send_sems.at[slot],
            recv_sem=recv_sems.at[slot],
            device_id={"head": partner},
            device_id_type=pl.DeviceIdType.MESH,
        )

    def partial(side, mask, store):
        first = (me ^ mask) * (2 * half) + side * half
        flip = anti_identity(tile)

        def one(j, carry):
            at = pl.multiple_of(first + j * tile, tile)
            mirrored = pl.multiple_of(depth - tile - at, tile)
            flipped = matmul(w_ref[:, pl.ds(mirrored, tile)], flip).astype(BF16)
            value = matmul(normed_ref[0], w_ref[:, pl.ds(at, tile)]) + matmul(
                normed_ref[1], flipped
            )
            store(pl.ds(pl.multiple_of(j * tile, tile), tile), value)
            return carry

        lax.fori_loop(0, half // tile, one, 0)

    def into_sending(slot):
        def store(columns, value):
            sending[slot, :, columns] = value.astype(BF16)

        return store

    def into_held(slot):
        def store(columns, value):
            held[slot, :, columns] = value

        return store

    pieces = sorted(
        ((phase_of(side, mask), -bin(mask).count("1"), mask, side)
         for side in range(2) for mask in range(1, count)),
        key=lambda piece: piece[:2],
    )
    later = [(side, mask) for phase, _, mask, side in pieces if phase > 0] + [(0, 0), (1, 0)]
    for phase, _, mask, side in pieces:
        if phase == 0:
            partial(side, mask, into_sending(side * (count - 1) + mask - 1))
            copy_of(side, mask).start()
    for place, (side, mask) in enumerate(later):
        partial(side, mask, into_held(place))
    for place, (side, mask) in enumerate(later):
        total = held[place]
        for q in range(phase_of(side, mask) if mask else bits):
            source = mask | 1 << orders[side][q]
            copy_of(side, source).wait_recv()
            total = total + landed[side * (count - 1) + source - 1].astype(F32)
        if mask:
            sending[side * (count - 1) + mask - 1] = total.astype(BF16)
            copy_of(side, mask).start()
        else:
            out_ref[:, side * half : (side + 1) * half] = total.astype(BF16)
    for _, _, mask, side in pieces:
        copy_of(side, mask).wait_send()


def project_out(normed, w_out):
    _, length, inner = normed.shape
    depth = w_out.shape[1]
    count = lax.axis_size("head")
    half = depth // count // 2
    slots = 2 * (count - 1)
    return pl.pallas_call(
        functools.partial(project_out_kernel, count),
        in_specs=[pl.BlockSpec(memory_space=pltpu.VMEM)] * 2,
        out_specs=pl.BlockSpec(memory_space=pltpu.VMEM),
        out_shape=jax.ShapeDtypeStruct((length, depth // count), BF16),
        scratch_shapes=[
            pltpu.VMEM((count, length, half), F32),
            pltpu.VMEM((slots, length, half), BF16),
            pltpu.VMEM((slots, length, half), BF16),
            pltpu.SemaphoreType.DMA((slots,)),
            pltpu.SemaphoreType.DMA((slots,)),
        ],
        compiler_params=pltpu.CompilerParams(
            vmem_limit_bytes=40 * 1024 * 1024, collective_id=0, has_side_effects=True
        ),
        name="project_out",
    )(normed, w_out)


def shards(
    hidden, base_ids, norm_gain, w_gate, w_value, w_bc, w_step, conv_value, conv_bc,
    step_bias, decay_rate, skip_gain, out_gain, w_out,
):
    keep = (base_ids != 4).astype(F32)[:, None]
    length, depth = hidden.shape
    inner = w_gate.shape[1]
    heads = w_step.shape[1]
    width = inner // heads
    chunks = inner // COLS
    per = COLS // width
    scaled, squares = prepare(hidden, norm_gain)
    inv_rms = lax.rsqrt(jnp.sum(squares, axis=-1) / depth + EPSILON)[:, None]

    def project(weight):
        return (
            jnp.einsum("btd,dk->btk", scaled, weight, preferred_element_type=F32) * inv_rms
        )

    bc_in = project(w_bc)
    step_in = project(w_step)
    value_in = project(w_value)
    size = lax.axis_size("ctx")
    up = [(i, i + 1) for i in range(size - 1)]
    down = [(i + 1, i) for i in range(size - 1)]
    tail = jnp.concatenate([value_in[:, length - HALO :], bc_in[:, length - HALO :]], axis=-1)
    head = jnp.concatenate([value_in[:, :HALO], bc_in[:, :HALO]], axis=-1)
    before = lax.ppermute(tail, "ctx", up)
    after = lax.ppermute(head, "ctx", down)
    gate_in = project(w_gate)

    steps = jax.nn.softplus(step_in + step_bias)
    log_decay = -decay_rate * steps
    lower = jnp.tril(jnp.ones((length, length), F32))
    triangles = jnp.stack([lower, lower.T])
    cum = jnp.einsum("dts,bsh->bdth", triangles, log_decay, precision=PRECISE)
    log_total = cum[:, 0, -1]
    packed = jnp.concatenate([cum, steps[:, None]], axis=1)
    packed = packed.reshape(2, 3, length, chunks, per)
    aux = packed.transpose(0, 3, 2, 1, 4).reshape(2, chunks, length, 3 * per)
    rows = packed[:, :2].transpose(0, 3, 1, 4, 2).reshape(2, chunks, 2 * per, length)

    x, bc, bt, local = mix(value_in, bc_in, before, after, conv_value, conv_bc, aux, keep)
    total = jnp.broadcast_to(jnp.repeat(log_total, width, axis=-1)[:, None], (2, 8, inner))
    y, entering = scan_local(
        x, bc, bt, aux, rows, jnp.repeat(skip_gain, width)[None], local, total
    )
    normed = finish(y, bc, entering, aux, gate_in, out_gain[None])
    return project_out(normed, w_out)


def solution(mesh):
    return jax.shard_map(
        shards,
        mesh=mesh,
        in_specs=(
            P("ctx", None),
            P("ctx"),
            P(),
            P(None, "head"),
            P(None, "head"),
            P(),
            P(None, "head"),
            P(None, "head"),
            P(),
            P("head"),
            P("head"),
            P("head"),
            P("head"),
            P("head", None),
        ),
        out_specs=P("ctx", "head"),
        check_vma=False,
    )
```

```python
import functools

import jax
import jax.numpy as jnp
from jax import lax
from jax.experimental import pallas as pl
from jax.experimental.pallas import tpu as pltpu
from jax.sharding import PartitionSpec as P

EPSILON = 1e-05
PRECISE = lax.Precision.HIGHEST
F32 = jnp.float32
BF16 = jnp.bfloat16
COLS = 256
ROWS = 128
HALO = 8
VMEM_LIMIT = 56 * 1024 * 1024


def params(dims):
    return pltpu.CompilerParams(
        vmem_limit_bytes=VMEM_LIMIT, dimension_semantics=("arbitrary",) * dims
    )


def anti_identity(size):
    row = lax.broadcasted_iota(jnp.int32, (size, size), 0)
    col = lax.broadcasted_iota(jnp.int32, (size, size), 1)
    return (row + col == size - 1).astype(F32).astype(BF16)


def matmul(a, b):
    return jnp.dot(a, b, preferred_element_type=F32)


def spread(per_head, width):
    heads = per_head.shape[1]
    high = per_head.astype(BF16)
    low = (per_head - high.astype(F32)).astype(BF16)
    row = lax.broadcasted_iota(jnp.int32, (2 * heads, heads * width), 0)
    col = lax.broadcasted_iota(jnp.int32, (2 * heads, heads * width), 1)
    row = jnp.where(row < heads, row, row - heads)
    pick = ((col >= row * width) & (col < (row + 1) * width)).astype(F32).astype(BF16)
    return matmul(jnp.concatenate([high, low], axis=1), pick)


def silu(x):
    half = 0.5 * x
    return half + half * jnp.tanh(half)


def prepare_kernel(own_ref, mirror_ref, gain_ref, scaled_ref, squares_ref):
    flip = anti_identity(COLS)
    parts = own_ref.shape[1] // COLS
    squares = None
    for q in range(parts):
        at = slice(q * COLS, (q + 1) * COLS)
        opposite = slice((parts - 1 - q) * COLS, (parts - q) * COLS)
        own = own_ref[:, at].astype(F32)
        gain = gain_ref[:, at]
        scaled_ref[0, :, at] = (own * gain).astype(BF16)
        scaled_ref[1, :, at] = (matmul(mirror_ref[:, opposite], flip) * gain).astype(BF16)
        square = own * own
        square = square[:, :128] + square[:, 128:]
        squares = square if squares is None else squares + square

    @pl.when(pl.program_id(0) == 0)
    def _():
        squares_ref[...] = squares

    @pl.when(pl.program_id(0) > 0)
    def _():
        squares_ref[...] += squares


def prepare(hidden, gain):
    length, depth = hidden.shape
    span = 4 * COLS
    count = depth // span
    return pl.pallas_call(
        prepare_kernel,
        grid=(count,),
        in_specs=[
            pl.BlockSpec((length, span), lambda j: (0, j)),
            pl.BlockSpec((length, span), lambda j: (0, count - 1 - j)),
            pl.BlockSpec((1, span), lambda j: (0, j)),
        ],
        out_specs=[
            pl.BlockSpec((2, length, span), lambda j: (0, 0, j)),
            pl.BlockSpec((length, 128), lambda j: (0, 0)),
        ],
        out_shape=[
            jax.ShapeDtypeStruct((2, length, depth), BF16),
            jax.ShapeDtypeStruct((length, 128), F32),
        ],
        compiler_params=params(1),
        name="prepare",
    )(hidden, hidden, gain[None])


def convolve(out, ext, main_ref, before_ref, after_ref, taps_ref):
    length = main_ref.shape[1]
    ext[0:HALO] = before_ref[0]
    ext[HALO : HALO + length] = main_ref[0]
    ext[HALO + length :] = after_ref[0]
    taps = [taps_ref[k : k + 1, :] for k in range(4)]
    step = 64
    for start in range(0, length, step):
        rows = [ext[start + HALO - 3 + k : start + HALO - 3 + k + step] for k in range(7)]
        forward = taps[0] * rows[0]
        backward = taps[0] * rows[6]
        for k in range(1, 4):
            forward = forward + taps[k] * rows[k]
            backward = backward + taps[k] * rows[6 - k]
        out(start, step, silu(forward), silu(backward))


def mix_kernel(
    v_ref, bc_ref, before_v, before_bc, after_v, after_bc, taps_v, taps_bc, aux_ref, keep_ref,
    x_ref, bco_ref, bt_ref, s_ref, ext,
):
    c = pl.program_id(1)
    length = v_ref.shape[1]

    @pl.when(c == 0)
    def _():
        def out(start, step, forward, backward):
            bco_ref[0, 0, start : start + step] = forward.astype(BF16)
            bco_ref[0, 1, start : start + step] = backward.astype(BF16)

        convolve(out, ext, bc_ref, before_bc, after_bc, taps_bc)
        state = bt_ref.shape[2]
        for d in range(2):
            bt_ref[0, d] = bco_ref[0, d, :, :state].astype(F32).T.astype(BF16)

    @pl.when(c > 0)
    def _():
        def out(start, step, forward, backward):
            keep = keep_ref[start : start + step]
            x_ref[0, 0, start : start + step] = (forward * keep).astype(BF16)
            x_ref[0, 1, start : start + step] = (backward * keep).astype(BF16)

        convolve(out, ext, v_ref, before_v, after_v, taps_v)
        heads = aux_ref.shape[3] // 3
        aux = aux_ref[0, 0]
        steps = aux[:, 2 * heads :]
        for d in range(2):
            cum = aux[:, d * heads : (d + 1) * heads]
            total = cum[length - 1 :] if d == 0 else cum[:1]
            weight = spread(jnp.exp(total - cum) * steps, COLS // heads)
            s_ref[0, d] = matmul(bt_ref[0, d], (x_ref[0, d].astype(F32) * weight).astype(BF16))


def mix(value_in, bc_in, before, after, conv_value, conv_bc, aux, keep):
    _, length, inner = value_in.shape
    pair = bc_in.shape[2]
    state = pair // 2
    chunks = inner // COLS
    before_v, before_bc = before[..., :inner], before[..., inner:]
    after_v, after_bc = after[..., :inner], after[..., inner:]

    def at(c):
        return jnp.maximum(c - 1, 0)

    return pl.pallas_call(
        mix_kernel,
        grid=(2, chunks + 1),
        in_specs=[
            pl.BlockSpec((1, length, COLS), lambda b, c: (b, 0, at(c))),
            pl.BlockSpec((1, length, pair), lambda b, c: (b, 0, 0)),
            pl.BlockSpec((1, HALO, COLS), lambda b, c: (b, 0, at(c))),
            pl.BlockSpec((1, HALO, pair), lambda b, c: (b, 0, 0)),
            pl.BlockSpec((1, HALO, COLS), lambda b, c: (b, 0, at(c))),
            pl.BlockSpec((1, HALO, pair), lambda b, c: (b, 0, 0)),
            pl.BlockSpec((4, COLS), lambda b, c: (0, at(c))),
            pl.BlockSpec((4, pair), lambda b, c: (0, 0)),
            pl.BlockSpec((1, 1) + aux.shape[2:], lambda b, c: (b, at(c), 0, 0)),
            pl.BlockSpec((length, 1), lambda b, c: (0, 0)),
        ],
        out_specs=[
            pl.BlockSpec((1, 2, length, COLS), lambda b, c: (b, 0, 0, at(c))),
            pl.BlockSpec((1, 2, length, pair), lambda b, c: (b, 0, 0, 0)),
            pl.BlockSpec((1, 2, state, length), lambda b, c: (b, 0, 0, 0)),
            pl.BlockSpec((1, 2, state, COLS), lambda b, c: (b, 0, 0, at(c))),
        ],
        out_shape=[
            jax.ShapeDtypeStruct((2, 2, length, inner), BF16),
            jax.ShapeDtypeStruct((2, 2, length, pair), BF16),
            jax.ShapeDtypeStruct((2, 2, state, length), BF16),
            jax.ShapeDtypeStruct((2, 2, state, inner), F32),
        ],
        scratch_shapes=[pltpu.VMEM((length + 2 * HALO, COLS), F32)],
        compiler_params=params(2),
        cost_estimate=pl.CostEstimate(
            flops=2 * 4 * length * state * inner,
            bytes_accessed=14 * 2 * length * inner,
            transcendentals=4 * length * inner,
        ),
        name="mix",
    )(value_in, bc_in, before_v, before_bc, after_v, after_bc, conv_value, conv_bc, aux, keep)


def chain(size, last, local_ref, total_ref, ent_ref, swapped, decay_other, chip, kept,
          hop_out, hop_in, crossed, send_sems, recv_sems):
    me = lax.axis_index("ctx")
    odd = lax.rem(me, 2)
    hops = size // 2 - 1
    ahead = me + 4 * odd - 2
    behind = me - 4 * odd + 2
    has_ahead = (ahead >= 0) & (ahead < size)
    has_behind = (behind >= 0) & (behind < size)
    partner = me + 1 - 2 * odd

    def remote(source, target, index, device):
        return pltpu.make_async_remote_copy(
            src_ref=source,
            dst_ref=target,
            send_sem=send_sems.at[index],
            recv_sem=recv_sems.at[index],
            device_id={"ctx": device},
            device_id_type=pl.DeviceIdType.MESH,
        )

    swap_copy = remote(kept, swapped, 0, partner)
    decay_copy = remote(total_ref, decay_other, 1, partner)
    cross_copy = remote(kept, crossed, 2, partner)
    hop_copies = [remote(hop_out.at[k], hop_in.at[k], 3 + k, ahead) for k in range(hops)]

    def greet():
        barrier = pltpu.get_barrier_semaphore()

        def signal(device):
            pl.semaphore_signal(
                barrier, inc=1, device_id={"ctx": device}, device_id_type=pl.DeviceIdType.MESH
            )

        signal(partner)
        pl.when(has_ahead)(lambda: signal(ahead))
        pl.when(has_behind)(lambda: signal(behind))
        pl.semaphore_wait(
            barrier, 1 + has_ahead.astype(jnp.int32) + has_behind.astype(jnp.int32)
        )

    def first():
        greet()
        for b in range(2):
            kept[b] = jnp.where(odd == 1, local_ref[b, 1], local_ref[b, 0]).astype(BF16)
        swap_copy.start()
        decay_copy.start()

    def second():
        swap_copy.wait()
        decay_copy.wait()
        for b in range(2):
            mine = jnp.where(odd == 1, local_ref[b, 0], local_ref[b, 1])
            decay = jnp.exp(total_ref[b, :1])
            chip[b] = decay * swapped[b].astype(F32) + mine
            hop_out[0, b] = chip[b].astype(BF16)
        pl.when(has_ahead)(lambda: hop_copies[0].start())

    def entered(k, b):
        return jnp.where(has_behind, hop_in[k, b].astype(F32), 0.0)

    def hop(k):
        def stage():
            pl.when(has_behind)(lambda: hop_copies[k - 1].wait_recv())
            for b in range(2):
                decay = jnp.exp(total_ref[b, :1] + decay_other[b, :1])
                hop_out[k, b] = (chip[b] + decay * entered(k - 1, b)).astype(BF16)
            pl.when(has_ahead)(lambda: hop_copies[k].start())

        return stage

    def cross():
        pl.when(has_behind)(lambda: hop_copies[hops - 1].wait_recv())
        for b in range(2):
            kept[b] = entered(hops - 1, b).astype(BF16)
        cross_copy.start()

    def end():
        cross_copy.wait()
        for b in range(2):
            own = jnp.exp(decay_other[b, :1]) * kept[b].astype(F32) + swapped[b].astype(F32)
            other = crossed[b].astype(F32)
            ent_ref[b, 0] = jnp.where(odd == 1, own, other).astype(BF16)
            ent_ref[b, 1] = jnp.where(odd == 1, other, own).astype(BF16)
        for k in range(hops):
            pl.when(has_ahead)(lambda k=k: hop_copies[k].wait_send())

    stages = [first, second] + [hop(k) for k in range(1, hops)] + [cross]
    return [(min(last, (7 * i) // 5), stage) for i, stage in enumerate(stages)], end


def scan_kernel(size, x_ref, bc_ref, bt_ref, aux_ref, row_ref, skip_ref, local_ref, total_ref,
                y_ref, ent_ref, *scratch):
    step = pl.program_id(0) * pl.num_programs(1) + pl.program_id(1)
    last_step = 2 * (local_ref.shape[3] // COLS) - 1
    stages, end = chain(size, last_step, local_ref, total_ref, ent_ref, *scratch)
    for at, stage in stages:
        pl.when(step == at)(stage)
    length = x_ref.shape[2]
    state = bt_ref.shape[2]
    heads = aux_ref.shape[3] // 3
    width = COLS // heads
    row = lax.broadcasted_iota(jnp.int32, (ROWS, ROWS), 0)
    col = lax.broadcasted_iota(jnp.int32, (ROWS, ROWS), 1)
    on_left = lax.broadcasted_iota(jnp.int32, (1, 2 * width), 1) < width
    left = on_left.astype(F32).astype(BF16)
    right = (1.0 - on_left.astype(F32)).astype(BF16)
    blocks = length // ROWS

    def diagonal(pair):
        return jnp.concatenate([pair * left, pair * right], axis=0)

    for d in range(2):
        carried = [None] * (heads // 2)
        reach = (row >= col) if d == 0 else (row <= col)
        order = range(blocks) if d == 0 else range(blocks - 1, -1, -1)
        for lap, i in enumerate(order):
            own = slice(i * ROWS, (i + 1) * ROWS)
            cum = aux_ref[0, 0, own, d * heads : (d + 1) * heads]
            lines = row_ref[0, 0, d * heads : (d + 1) * heads, own]
            c_rows = bc_ref[0, d, own, state:]
            c_wide = c_rows.astype(F32)
            b_wide = bt_ref[0, d, :, own].astype(F32)
            scores = lax.dot_general(
                c_rows, bc_ref[0, d, own, :state], (((1,), (1,)), ((), ())),
                preferred_element_type=F32,
            )
            final = cum[ROWS - 1 :] if d == 0 else cum[:1]
            if lap > 0:
                entry = (i * ROWS - 1) if d == 0 else (i + 1) * ROWS
                base = aux_ref[0, 0, entry : entry + 1, d * heads : (d + 1) * heads]
            for p in range(heads // 2):
                weights, tails, entries, decays = [], [], [], []
                for h in (2 * p, 2 * p + 1):
                    tall = jnp.broadcast_to(cum[:, h : h + 1], (ROWS, ROWS))
                    line = lines[h : h + 1]
                    gap = jnp.where(reach, tall - line, -jnp.inf)
                    weights.append((jnp.exp(gap) * scores).astype(BF16))
                    if lap < blocks - 1:
                        tails.append((b_wide * jnp.exp(final[:, h : h + 1] - line)).astype(BF16))
                    if lap > 0:
                        start = base[:, h : h + 1]
                        entries.append((c_wide * jnp.exp(tall - start)).astype(BF16))
                        decays.append(jnp.exp(final[:, h : h + 1] - start))
                at = slice(2 * p * width, 2 * (p + 1) * width)
                x = x_ref[0, d, own, at]
                lhs = jnp.concatenate(weights, axis=1)
                if tails:
                    lhs = jnp.concatenate([lhs, jnp.concatenate(tails, axis=1)], axis=0)
                result = matmul(lhs, diagonal(x))
                local = result[:ROWS] + skip_ref[:, at] * x.astype(F32)
                if entries:
                    local = local + matmul(
                        jnp.concatenate(entries, axis=1), diagonal(carried[p].astype(BF16))
                    )
                if tails:
                    fresh = result[ROWS:]
                    if entries:
                        fresh = jnp.where(on_left, decays[0], decays[1]) * carried[p] + fresh
                    carried[p] = fresh
                if d == 0:
                    y_ref[0, own, at] = local
                else:
                    y_ref[0, own, at] += local
    pl.when(step == last_step)(end)


def scan_local(x, bc, bt, aux, rows, skip, local, total):
    size = lax.axis_size("ctx")
    hops = size // 2 - 1
    wide = local.shape[2:]
    _, _, length, inner = x.shape
    pair = bc.shape[3]
    state = pair // 2
    chunks = inner // COLS
    return pl.pallas_call(
        functools.partial(scan_kernel, size),
        grid=(2, chunks),
        in_specs=[
            pl.BlockSpec((1, 2, length, COLS), lambda b, c: (b, 0, 0, c)),
            pl.BlockSpec((1, 2, length, pair), lambda b, c: (b, 0, 0, 0)),
            pl.BlockSpec((1, 2, state, length), lambda b, c: (b, 0, 0, 0)),
            pl.BlockSpec((1, 1) + aux.shape[2:], lambda b, c: (b, c, 0, 0)),
            pl.BlockSpec((1, 1) + rows.shape[2:], lambda b, c: (b, c, 0, 0)),
            pl.BlockSpec((1, COLS), lambda b, c: (0, c)),
            pl.BlockSpec(local.shape, lambda b, c: (0, 0, 0, 0)),
            pl.BlockSpec(total.shape, lambda b, c: (0, 0, 0)),
        ],
        out_specs=[
            pl.BlockSpec((1, length, COLS), lambda b, c: (b, 0, c)),
            pl.BlockSpec(local.shape, lambda b, c: (0, 0, 0, 0)),
        ],
        out_shape=[
            jax.ShapeDtypeStruct((2, length, inner), F32),
            jax.ShapeDtypeStruct(local.shape, BF16),
        ],
        scratch_shapes=[
            pltpu.VMEM((2,) + wide, BF16),
            pltpu.VMEM(total.shape, F32),
            pltpu.VMEM((2,) + wide, F32),
            pltpu.VMEM((2,) + wide, BF16),
            pltpu.VMEM((hops, 2) + wide, BF16),
            pltpu.VMEM((hops, 2) + wide, BF16),
            pltpu.VMEM((2,) + wide, BF16),
            pltpu.SemaphoreType.DMA((3 + hops,)),
            pltpu.SemaphoreType.DMA((3 + hops,)),
        ],
        compiler_params=pltpu.CompilerParams(
            vmem_limit_bytes=VMEM_LIMIT,
            dimension_semantics=("arbitrary",) * 2,
            collective_id=1,
            has_side_effects=True,
        ),
        cost_estimate=pl.CostEstimate(
            flops=2 * 64 * length * ROWS * inner,
            bytes_accessed=20 * length * inner,
            transcendentals=0,
        ),
        name="scan_local",
    )(x, bc, bt, aux, rows, skip, local, total)


def finish_kernel(y_ref, bc_ref, s_ref, aux_ref, gate_ref, gain_ref, out_ref):
    state = s_ref.shape[2]
    heads = aux_ref.shape[3] // 3
    width = COLS // heads
    row = lax.broadcasted_iota(jnp.int32, (COLS, COLS), 0)
    col = lax.broadcasted_iota(jnp.int32, (COLS, COLS), 1)
    same = None
    for h in range(heads):
        low, high = h * width, (h + 1) * width
        square = (row >= low) & (row < high) & (col >= low) & (col < high)
        same = square if same is None else same | square
    same = same.astype(F32).astype(BF16)
    length = y_ref.shape[1]
    for start in range(0, length, 2 * ROWS):
        own = slice(start, start + 2 * ROWS)
        aux = aux_ref[0, 0, own]
        y = y_ref[0, own]
        for d in range(2):
            grown = spread(jnp.exp(aux[:, d * heads : (d + 1) * heads]), width)
            y = y + grown * matmul(bc_ref[0, d, own, state:], s_ref[0, d])
        gated = y * silu(gate_ref[0, own])
        mean = matmul((gated * gated).astype(BF16), same) * (1.0 / width)
        out_ref[0, own] = (gated * lax.rsqrt(mean + EPSILON) * gain_ref[...]).astype(BF16)


def finish(y, bc, entering, aux, gate_in, gain):
    _, length, inner = y.shape
    pair = bc.shape[3]
    chunks = inner // COLS
    return pl.pallas_call(
        finish_kernel,
        grid=(2, chunks),
        in_specs=[
            pl.BlockSpec((1, length, COLS), lambda b, c: (b, 0, c)),
            pl.BlockSpec((1, 2, length, pair), lambda b, c: (b, 0, 0, 0)),
            pl.BlockSpec((1, 2, pair // 2, COLS), lambda b, c: (b, 0, 0, c)),
            pl.BlockSpec((1, 1) + aux.shape[2:], lambda b, c: (b, c, 0, 0)),
            pl.BlockSpec((1, length, COLS), lambda b, c: (b, 0, c)),
            pl.BlockSpec((1, COLS), lambda b, c: (0, c)),
        ],
        out_specs=pl.BlockSpec((1, length, COLS), lambda b, c: (b, 0, c)),
        out_shape=jax.ShapeDtypeStruct((2, length, inner), BF16),
        compiler_params=params(2),
        name="finish",
    )(y, bc, entering, aux, gate_in, gain)


def project_out_kernel(
    count, normed_ref, w_ref, out_ref, held, sending, landed, send_sems, recv_sems
):
    me = lax.axis_index("head")
    bits = count.bit_length() - 1
    inner, depth = w_ref.shape
    half = depth // count // 2
    tile = min(half, COLS)
    orders = (list(range(bits)), list(range(bits))[::-1])

    barrier = pltpu.get_barrier_semaphore()
    for bit in range(bits):
        pl.semaphore_signal(
            barrier, inc=1, device_id={"head": me ^ (1 << bit)},
            device_id_type=pl.DeviceIdType.MESH,
        )
    pl.semaphore_wait(barrier, bits)

    def phase_of(side, mask):
        return next(p for p, bit in enumerate(orders[side]) if mask >> bit & 1)

    def copy_of(side, mask):
        slot = side * (count - 1) + mask - 1
        partner = me ^ (1 << orders[side][phase_of(side, mask)])
        return pltpu.make_async_remote_copy(
            src_ref=sending.at[slot],
            dst_ref=landed.at[slot],
            send_sem=send_sems.at[slot],
            recv_sem=recv_sems.at[slot],
            device_id={"head": partner},
            device_id_type=pl.DeviceIdType.MESH,
        )

    def partial(side, mask, store):
        first = (me ^ mask) * (2 * half) + side * half
        flip = anti_identity(tile)

        def one(j, carry):
            at = pl.multiple_of(first + j * tile, tile)
            mirrored = pl.multiple_of(depth - tile - at, tile)
            flipped = matmul(w_ref[:, pl.ds(mirrored, tile)], flip).astype(BF16)
            value = matmul(normed_ref[0], w_ref[:, pl.ds(at, tile)]) + matmul(
                normed_ref[1], flipped
            )
            store(pl.ds(pl.multiple_of(j * tile, tile), tile), value)
            return carry

        lax.fori_loop(0, half // tile, one, 0)

    def into_sending(slot):
        def store(columns, value):
            sending[slot, :, columns] = value.astype(BF16)

        return store

    def into_held(slot):
        def store(columns, value):
            held[slot, :, columns] = value

        return store

    pieces = sorted(
        ((phase_of(side, mask), -bin(mask).count("1"), mask, side)
         for side in range(2) for mask in range(1, count)),
        key=lambda piece: piece[:2],
    )
    later = [(side, mask) for phase, _, mask, side in pieces if phase > 0] + [(0, 0), (1, 0)]
    for phase, _, mask, side in pieces:
        if phase == 0:
            partial(side, mask, into_sending(side * (count - 1) + mask - 1))
            copy_of(side, mask).start()
    for place, (side, mask) in enumerate(later):
        partial(side, mask, into_held(place))
    for place, (side, mask) in enumerate(later):
        total = held[place]
        for q in range(phase_of(side, mask) if mask else bits):
            source = mask | 1 << orders[side][q]
            copy_of(side, source).wait_recv()
            total = total + landed[side * (count - 1) + source - 1].astype(F32)
        if mask:
            sending[side * (count - 1) + mask - 1] = total.astype(BF16)
            copy_of(side, mask).start()
        else:
            out_ref[:, side * half : (side + 1) * half] = total.astype(BF16)
    for _, _, mask, side in pieces:
        copy_of(side, mask).wait_send()


def project_out(normed, w_out):
    _, length, inner = normed.shape
    depth = w_out.shape[1]
    count = lax.axis_size("head")
    half = depth // count // 2
    slots = 2 * (count - 1)
    return pl.pallas_call(
        functools.partial(project_out_kernel, count),
        in_specs=[pl.BlockSpec(memory_space=pltpu.VMEM)] * 2,
        out_specs=pl.BlockSpec(memory_space=pltpu.VMEM),
        out_shape=jax.ShapeDtypeStruct((length, depth // count), BF16),
        scratch_shapes=[
            pltpu.VMEM((count, length, half), F32),
            pltpu.VMEM((slots, length, half), BF16),
            pltpu.VMEM((slots, length, half), BF16),
            pltpu.SemaphoreType.DMA((slots,)),
            pltpu.SemaphoreType.DMA((slots,)),
        ],
        compiler_params=pltpu.CompilerParams(
            vmem_limit_bytes=40 * 1024 * 1024, collective_id=0, has_side_effects=True
        ),
        name="project_out",
    )(normed, w_out)


def shards(
    hidden, base_ids, norm_gain, w_gate, w_value, w_bc, w_step, conv_value, conv_bc,
    step_bias, decay_rate, skip_gain, out_gain, w_out,
):
    keep = (base_ids != 4).astype(F32)[:, None]
    length, depth = hidden.shape
    inner = w_gate.shape[1]
    heads = w_step.shape[1]
    width = inner // heads
    chunks = inner // COLS
    per = COLS // width
    scaled, squares = prepare(hidden, norm_gain)
    inv_rms = lax.rsqrt(jnp.sum(squares, axis=-1) / depth + EPSILON)[:, None]

    def project(weight):
        return (
            jnp.einsum("btd,dk->btk", scaled, weight, preferred_element_type=F32) * inv_rms
        )

    bc_in = project(w_bc)
    step_in = project(w_step)
    value_in = project(w_value)
    size = lax.axis_size("ctx")
    up = [(i, i + 1) for i in range(size - 1)]
    down = [(i + 1, i) for i in range(size - 1)]
    tail = jnp.concatenate([value_in[:, length - HALO :], bc_in[:, length - HALO :]], axis=-1)
    head = jnp.concatenate([value_in[:, :HALO], bc_in[:, :HALO]], axis=-1)
    before = lax.ppermute(tail, "ctx", up)
    after = lax.ppermute(head, "ctx", down)
    gate_in = project(w_gate)

    steps = jax.nn.softplus(step_in + step_bias)
    log_decay = -decay_rate * steps
    lower = jnp.tril(jnp.ones((length, length), F32))
    triangles = jnp.stack([lower, lower.T])
    cum = jnp.einsum("dts,bsh->bdth", triangles, log_decay, precision=PRECISE)
    log_total = cum[:, 0, -1]
    packed = jnp.concatenate([cum, steps[:, None]], axis=1)
    packed = packed.reshape(2, 3, length, chunks, per)
    aux = packed.transpose(0, 3, 2, 1, 4).reshape(2, chunks, length, 3 * per)
    lines = (cum - jnp.log(steps)[:, None]).reshape(2, 2, length, chunks, per)
    rows = lines.transpose(0, 3, 1, 4, 2).reshape(2, chunks, 2 * per, length)

    x, bc, bt, local = mix(value_in, bc_in, before, after, conv_value, conv_bc, aux, keep)
    total = jnp.broadcast_to(jnp.repeat(log_total, width, axis=-1)[:, None], (2, 8, inner))
    y, entering = scan_local(
        x, bc, bt, aux, rows, jnp.repeat(skip_gain, width)[None], local, total
    )
    normed = finish(y, bc, entering, aux, gate_in, out_gain[None])
    return project_out(normed, w_out)


def solution(mesh):
    return jax.shard_map(
        shards,
        mesh=mesh,
        in_specs=(
            P("ctx", None),
            P("ctx"),
            P(),
            P(None, "head"),
            P(None, "head"),
            P(),
            P(None, "head"),
            P(None, "head"),
            P(),
            P("head"),
            P("head"),
            P("head"),
            P("head"),
            P("head", None),
        ),
        out_specs=P("ctx", "head"),
        check_vma=False,
    )
```

```python
import functools

import jax
import jax.numpy as jnp
from jax import lax
from jax.experimental import pallas as pl
from jax.experimental.pallas import tpu as pltpu
from jax.sharding import PartitionSpec as P

EPSILON = 1e-05
PRECISE = lax.Precision.HIGHEST
F32 = jnp.float32
BF16 = jnp.bfloat16
COLS = 256
ROWS = 128
HALO = 8
MIB = 1024 * 1024


def params(dims, mib):
    return pltpu.CompilerParams(
        vmem_limit_bytes=mib * MIB, dimension_semantics=("arbitrary",) * dims
    )


def anti_identity(size):
    row = lax.broadcasted_iota(jnp.int32, (size, size), 0)
    col = lax.broadcasted_iota(jnp.int32, (size, size), 1)
    return (row + col == size - 1).astype(F32).astype(BF16)


def matmul(a, b):
    return jnp.dot(a, b, preferred_element_type=F32)


def spread(per_head, width):
    heads = per_head.shape[1]
    high = per_head.astype(BF16)
    low = (per_head - high.astype(F32)).astype(BF16)
    row = lax.broadcasted_iota(jnp.int32, (2 * heads, heads * width), 0)
    col = lax.broadcasted_iota(jnp.int32, (2 * heads, heads * width), 1)
    row = jnp.where(row < heads, row, row - heads)
    pick = ((col >= row * width) & (col < (row + 1) * width)).astype(F32).astype(BF16)
    return matmul(jnp.concatenate([high, low], axis=1), pick)


def silu(x):
    half = 0.5 * x
    return half + half * jnp.tanh(half)


def prepare_kernel(own_ref, mirror_ref, gain_ref, scaled_ref, squares_ref):
    flip = anti_identity(COLS)
    parts = own_ref.shape[1] // COLS
    squares = None
    for q in range(parts):
        at = slice(q * COLS, (q + 1) * COLS)
        opposite = slice((parts - 1 - q) * COLS, (parts - q) * COLS)
        own = own_ref[:, at].astype(F32)
        gain = gain_ref[:, at]
        scaled_ref[0, :, at] = (own * gain).astype(BF16)
        scaled_ref[1, :, at] = (matmul(mirror_ref[:, opposite], flip) * gain).astype(BF16)
        square = own * own
        square = square[:, :128] + square[:, 128:]
        squares = square if squares is None else squares + square

    @pl.when(pl.program_id(0) == 0)
    def _():
        squares_ref[...] = squares

    @pl.when(pl.program_id(0) > 0)
    def _():
        squares_ref[...] += squares


def prepare(hidden, gain):
    length, depth = hidden.shape
    span = 4 * COLS
    count = depth // span
    return pl.pallas_call(
        prepare_kernel,
        grid=(count,),
        in_specs=[
            pl.BlockSpec((length, span), lambda j: (0, j)),
            pl.BlockSpec((length, span), lambda j: (0, count - 1 - j)),
            pl.BlockSpec((1, span), lambda j: (0, j)),
        ],
        out_specs=[
            pl.BlockSpec((2, length, span), lambda j: (0, 0, j)),
            pl.BlockSpec((length, 128), lambda j: (0, 0)),
        ],
        out_shape=[
            jax.ShapeDtypeStruct((2, length, depth), BF16),
            jax.ShapeDtypeStruct((length, 128), F32),
        ],
        compiler_params=params(1, 20),
        name="prepare",
    )(hidden, hidden, gain[None])


def convolve(out, ext, main_ref, before_ref, after_ref, taps_ref):
    length = main_ref.shape[1]
    ext[0:HALO] = before_ref[0]
    ext[HALO : HALO + length] = main_ref[0]
    ext[HALO + length :] = after_ref[0]
    taps = [taps_ref[k : k + 1, :] for k in range(4)]
    step = 64
    for start in range(0, length, step):
        rows = [ext[start + HALO - 3 + k : start + HALO - 3 + k + step] for k in range(7)]
        forward = taps[0] * rows[0]
        backward = taps[0] * rows[6]
        for k in range(1, 4):
            forward = forward + taps[k] * rows[k]
            backward = backward + taps[k] * rows[6 - k]
        out(start, step, silu(forward), silu(backward))


def mix_kernel(
    v_ref, bc_ref, before_v, before_bc, after_v, after_bc, taps_v, taps_bc, aux_ref, keep_ref,
    x_ref, bco_ref, bt_ref, s_ref, ext,
):
    c = pl.program_id(1)
    length = v_ref.shape[1]

    @pl.when(c == 0)
    def _():
        def out(start, step, forward, backward):
            bco_ref[0, 0, start : start + step] = forward.astype(BF16)
            bco_ref[0, 1, start : start + step] = backward.astype(BF16)

        convolve(out, ext, bc_ref, before_bc, after_bc, taps_bc)
        state = bt_ref.shape[2]
        for d in range(2):
            bt_ref[0, d] = bco_ref[0, d, :, :state].astype(F32).T.astype(BF16)

    @pl.when(c > 0)
    def _():
        def out(start, step, forward, backward):
            keep = keep_ref[start : start + step]
            x_ref[0, 0, start : start + step] = (forward * keep).astype(BF16)
            x_ref[0, 1, start : start + step] = (backward * keep).astype(BF16)

        convolve(out, ext, v_ref, before_v, after_v, taps_v)
        heads = aux_ref.shape[3] // 3
        aux = aux_ref[0, 0]
        steps = aux[:, 2 * heads :]
        for d in range(2):
            cum = aux[:, d * heads : (d + 1) * heads]
            total = cum[length - 1 :] if d == 0 else cum[:1]
            weight = spread(jnp.exp(total - cum) * steps, COLS // heads)
            s_ref[0, d] = matmul(bt_ref[0, d], (x_ref[0, d].astype(F32) * weight).astype(BF16))


def mix(value_in, bc_in, before, after, conv_value, conv_bc, aux, keep):
    _, length, inner = value_in.shape
    pair = bc_in.shape[2]
    state = pair // 2
    chunks = inner // COLS
    before_v, before_bc = before[..., :inner], before[..., inner:]
    after_v, after_bc = after[..., :inner], after[..., inner:]

    def at(c):
        return jnp.maximum(c - 1, 0)

    return pl.pallas_call(
        mix_kernel,
        grid=(2, chunks + 1),
        in_specs=[
            pl.BlockSpec((1, length, COLS), lambda b, c: (b, 0, at(c))),
            pl.BlockSpec((1, length, pair), lambda b, c: (b, 0, 0)),
            pl.BlockSpec((1, HALO, COLS), lambda b, c: (b, 0, at(c))),
            pl.BlockSpec((1, HALO, pair), lambda b, c: (b, 0, 0)),
            pl.BlockSpec((1, HALO, COLS), lambda b, c: (b, 0, at(c))),
            pl.BlockSpec((1, HALO, pair), lambda b, c: (b, 0, 0)),
            pl.BlockSpec((4, COLS), lambda b, c: (0, at(c))),
            pl.BlockSpec((4, pair), lambda b, c: (0, 0)),
            pl.BlockSpec((1, 1) + aux.shape[2:], lambda b, c: (b, at(c), 0, 0)),
            pl.BlockSpec((length, 1), lambda b, c: (0, 0)),
        ],
        out_specs=[
            pl.BlockSpec((1, 2, length, COLS), lambda b, c: (b, 0, 0, at(c))),
            pl.BlockSpec((1, 2, length, pair), lambda b, c: (b, 0, 0, 0)),
            pl.BlockSpec((1, 2, state, length), lambda b, c: (b, 0, 0, 0)),
            pl.BlockSpec((1, 2, state, COLS), lambda b, c: (b, 0, 0, at(c))),
        ],
        out_shape=[
            jax.ShapeDtypeStruct((2, 2, length, inner), BF16),
            jax.ShapeDtypeStruct((2, 2, length, pair), BF16),
            jax.ShapeDtypeStruct((2, 2, state, length), BF16),
            jax.ShapeDtypeStruct((2, 2, state, inner), F32),
        ],
        scratch_shapes=[pltpu.VMEM((length + 2 * HALO, COLS), F32)],
        compiler_params=params(2, 16),
        cost_estimate=pl.CostEstimate(
            flops=2 * 4 * length * state * inner,
            bytes_accessed=14 * 2 * length * inner,
            transcendentals=4 * length * inner,
        ),
        name="mix",
    )(value_in, bc_in, before_v, before_bc, after_v, after_bc, conv_value, conv_bc, aux, keep)


def chain(size, last, local_ref, total_ref, ent_ref, swapped, decay_other, chip, kept,
          hop_out, hop_in, crossed, send_sems, recv_sems):
    me = lax.axis_index("ctx")
    odd = lax.rem(me, 2)
    ahead = me + 4 * odd - 2
    behind = me - 4 * odd + 2
    has_ahead = (ahead >= 0) & (ahead < size)
    has_behind = (behind >= 0) & (behind < size)
    partner = me + 1 - 2 * odd
    place = me // 2 * (2 * odd - 1) + (1 - odd) * (size // 2 - 1)

    def remote(source, target, index, device):
        return pltpu.make_async_remote_copy(
            src_ref=source,
            dst_ref=target,
            send_sem=send_sems.at[index],
            recv_sem=recv_sems.at[index],
            device_id={"ctx": device},
            device_id_type=pl.DeviceIdType.MESH,
        )

    swap_copy = remote(kept, swapped, 0, partner)
    decay_copy = remote(total_ref, decay_other, 1, partner)
    cross_copies = [remote(kept.at[b], crossed.at[b], 2 + b, partner) for b in range(2)]
    hop_copies = [remote(hop_out.at[b], hop_in.at[b], 4 + b, ahead) for b in range(2)]

    def greet():
        barrier = pltpu.get_barrier_semaphore()

        def signal(device):
            pl.semaphore_signal(
                barrier, inc=1, device_id={"ctx": device}, device_id_type=pl.DeviceIdType.MESH
            )

        signal(partner)
        pl.when(has_ahead)(lambda: signal(ahead))
        pl.when(has_behind)(lambda: signal(behind))
        pl.semaphore_wait(
            barrier, 1 + has_ahead.astype(jnp.int32) + has_behind.astype(jnp.int32)
        )

    def first():
        greet()
        for b in range(2):
            kept[b] = jnp.where(odd == 1, local_ref[b, 1], local_ref[b, 0]).astype(BF16)
        swap_copy.start()
        decay_copy.start()

    def second():
        swap_copy.wait()
        decay_copy.wait()
        for b in range(2):
            mine = jnp.where(odd == 1, local_ref[b, 0], local_ref[b, 1])
            decay = jnp.exp(total_ref[b, :1])
            chip[b] = decay * swapped[b].astype(F32) + mine

    def link(b):
        def stage():
            pl.when(has_behind)(lambda: hop_copies[b].wait_recv())
            decay = jnp.exp(total_ref[b, :1] + decay_other[b, :1])
            entering = jnp.where(has_behind, hop_in[b].astype(F32), 0.0)
            hop_out[b] = (chip[b] + decay * entering).astype(BF16)
            pl.when(has_ahead)(lambda: hop_copies[b].start())
            kept[b] = entering.astype(BF16)
            cross_copies[b].start()

        return stage

    def end():
        for b in range(2):
            cross_copies[b].wait()
            own = jnp.exp(decay_other[b, :1]) * kept[b].astype(F32) + swapped[b].astype(F32)
            other = crossed[b].astype(F32)
            ent_ref[b, 0] = jnp.where(odd == 1, own, other).astype(BF16)
            ent_ref[b, 1] = jnp.where(odd == 1, other, own).astype(BF16)
            pl.when(has_ahead)(lambda b=b: hop_copies[b].wait_send())

    stages = [(0, first), (1, second)]
    stages += [(jnp.minimum(place + b + 1, last), link(b)) for b in range(2)]
    return stages, end


def scan_kernel(size, x_ref, bc_ref, bt_ref, aux_ref, row_ref, skip_ref, local_ref, total_ref,
                y_ref, ent_ref, *scratch):
    step = pl.program_id(0) * pl.num_programs(1) + pl.program_id(1)
    last_step = 2 * (local_ref.shape[3] // COLS) - 1
    stages, end = chain(size, last_step, local_ref, total_ref, ent_ref, *scratch)
    for at, stage in stages:
        pl.when(step == at)(stage)
    length = x_ref.shape[2]
    state = bt_ref.shape[2]
    heads = aux_ref.shape[3] // 3
    width = COLS // heads
    row = lax.broadcasted_iota(jnp.int32, (ROWS, ROWS), 0)
    col = lax.broadcasted_iota(jnp.int32, (ROWS, ROWS), 1)
    on_left = lax.broadcasted_iota(jnp.int32, (1, 2 * width), 1) < width
    left = on_left.astype(F32).astype(BF16)
    right = (1.0 - on_left.astype(F32)).astype(BF16)
    blocks = length // ROWS

    def diagonal(pair):
        return jnp.concatenate([pair * left, pair * right], axis=0)

    for d in range(2):
        carried = [None] * (heads // 2)
        reach = (row >= col) if d == 0 else (row <= col)
        order = range(blocks) if d == 0 else range(blocks - 1, -1, -1)
        for lap, i in enumerate(order):
            own = slice(i * ROWS, (i + 1) * ROWS)
            cum = aux_ref[0, 0, own, d * heads : (d + 1) * heads]
            lines = row_ref[0, 0, d * heads : (d + 1) * heads, own]
            c_rows = bc_ref[0, d, own, state:]
            c_wide = c_rows.astype(F32)
            b_wide = bt_ref[0, d, :, own].astype(F32)
            scores = lax.dot_general(
                c_rows, bc_ref[0, d, own, :state], (((1,), (1,)), ((), ())),
                preferred_element_type=F32,
            )
            final = cum[ROWS - 1 :] if d == 0 else cum[:1]
            if lap > 0:
                entry = (i * ROWS - 1) if d == 0 else (i + 1) * ROWS
                base = aux_ref[0, 0, entry : entry + 1, d * heads : (d + 1) * heads]
            for p in range(heads // 2):
                weights, tails, entries, decays = [], [], [], []
                for h in (2 * p, 2 * p + 1):
                    tall = jnp.broadcast_to(cum[:, h : h + 1], (ROWS, ROWS))
                    line = lines[h : h + 1]
                    gap = jnp.where(reach, tall - line, -jnp.inf)
                    weights.append((jnp.exp(gap) * scores).astype(BF16))
                    if lap < blocks - 1:
                        tails.append((b_wide * jnp.exp(final[:, h : h + 1] - line)).astype(BF16))
                    if lap > 0:
                        start = base[:, h : h + 1]
                        entries.append((c_wide * jnp.exp(tall - start)).astype(BF16))
                        decays.append(jnp.exp(final[:, h : h + 1] - start))
                at = slice(2 * p * width, 2 * (p + 1) * width)
                x = x_ref[0, d, own, at]
                lhs = jnp.concatenate(weights, axis=1)
                if tails:
                    lhs = jnp.concatenate([lhs, jnp.concatenate(tails, axis=1)], axis=0)
                result = matmul(lhs, diagonal(x))
                local = result[:ROWS] + skip_ref[:, at] * x.astype(F32)
                if entries:
                    local = local + matmul(
                        jnp.concatenate(entries, axis=1), diagonal(carried[p].astype(BF16))
                    )
                if tails:
                    fresh = result[ROWS:]
                    if entries:
                        fresh = jnp.where(on_left, decays[0], decays[1]) * carried[p] + fresh
                    carried[p] = fresh
                if d == 0:
                    y_ref[0, own, at] = local
                else:
                    y_ref[0, own, at] += local
    pl.when(step == last_step)(end)


def scan_local(x, bc, bt, aux, rows, skip, local, total):
    size = lax.axis_size("ctx")
    wide = local.shape[2:]
    _, _, length, inner = x.shape
    pair = bc.shape[3]
    state = pair // 2
    chunks = inner // COLS
    return pl.pallas_call(
        functools.partial(scan_kernel, size),
        grid=(2, chunks),
        in_specs=[
            pl.BlockSpec((1, 2, length, COLS), lambda b, c: (b, 0, 0, c)),
            pl.BlockSpec((1, 2, length, pair), lambda b, c: (b, 0, 0, 0)),
            pl.BlockSpec((1, 2, state, length), lambda b, c: (b, 0, 0, 0)),
            pl.BlockSpec((1, 1) + aux.shape[2:], lambda b, c: (b, c, 0, 0)),
            pl.BlockSpec((1, 1) + rows.shape[2:], lambda b, c: (b, c, 0, 0)),
            pl.BlockSpec((1, COLS), lambda b, c: (0, c)),
            pl.BlockSpec(local.shape, lambda b, c: (0, 0, 0, 0)),
            pl.BlockSpec(total.shape, lambda b, c: (0, 0, 0)),
        ],
        out_specs=[
            pl.BlockSpec((1, length, COLS), lambda b, c: (b, 0, c)),
            pl.BlockSpec(local.shape, lambda b, c: (0, 0, 0, 0)),
        ],
        out_shape=[
            jax.ShapeDtypeStruct((2, length, inner), F32),
            jax.ShapeDtypeStruct(local.shape, BF16),
        ],
        scratch_shapes=[
            pltpu.VMEM((2,) + wide, BF16),
            pltpu.VMEM(total.shape, F32),
            pltpu.VMEM((2,) + wide, F32),
            pltpu.VMEM((2,) + wide, BF16),
            pltpu.VMEM((2,) + wide, BF16),
            pltpu.VMEM((2,) + wide, BF16),
            pltpu.VMEM((2,) + wide, BF16),
            pltpu.SemaphoreType.DMA((6,)),
            pltpu.SemaphoreType.DMA((6,)),
        ],
        compiler_params=pltpu.CompilerParams(
            vmem_limit_bytes=28 * MIB,
            dimension_semantics=("arbitrary",) * 2,
            collective_id=1,
            has_side_effects=True,
        ),
        cost_estimate=pl.CostEstimate(
            flops=2 * 64 * length * ROWS * inner,
            bytes_accessed=20 * length * inner,
            transcendentals=0,
        ),
        name="scan_local",
    )(x, bc, bt, aux, rows, skip, local, total)


def finish_kernel(y_ref, bc_ref, s_ref, aux_ref, gate_ref, gain_ref, out_ref):
    state = s_ref.shape[2]
    heads = aux_ref.shape[3] // 3
    width = COLS // heads
    row = lax.broadcasted_iota(jnp.int32, (COLS, COLS), 0)
    col = lax.broadcasted_iota(jnp.int32, (COLS, COLS), 1)
    same = None
    for h in range(heads):
        low, high = h * width, (h + 1) * width
        square = (row >= low) & (row < high) & (col >= low) & (col < high)
        same = square if same is None else same | square
    same = same.astype(F32).astype(BF16)
    length = y_ref.shape[1]
    for start in range(0, length, 2 * ROWS):
        own = slice(start, start + 2 * ROWS)
        aux = aux_ref[0, 0, own]
        y = y_ref[0, own]
        for d in range(2):
            grown = spread(jnp.exp(aux[:, d * heads : (d + 1) * heads]), width)
            y = y + grown * matmul(bc_ref[0, d, own, state:], s_ref[0, d])
        gated = y * silu(gate_ref[0, own])
        mean = matmul((gated * gated).astype(BF16), same) * (1.0 / width)
        out_ref[0, own] = (gated * lax.rsqrt(mean + EPSILON) * gain_ref[...]).astype(BF16)


def finish(y, bc, entering, aux, gate_in, gain):
    _, length, inner = y.shape
    pair = bc.shape[3]
    chunks = inner // COLS
    return pl.pallas_call(
        finish_kernel,
        grid=(2, chunks),
        in_specs=[
            pl.BlockSpec((1, length, COLS), lambda b, c: (b, 0, c)),
            pl.BlockSpec((1, 2, length, pair), lambda b, c: (b, 0, 0, 0)),
            pl.BlockSpec((1, 2, pair // 2, COLS), lambda b, c: (b, 0, 0, c)),
            pl.BlockSpec((1, 1) + aux.shape[2:], lambda b, c: (b, c, 0, 0)),
            pl.BlockSpec((1, length, COLS), lambda b, c: (b, 0, c)),
            pl.BlockSpec((1, COLS), lambda b, c: (0, c)),
        ],
        out_specs=pl.BlockSpec((1, length, COLS), lambda b, c: (b, 0, c)),
        out_shape=jax.ShapeDtypeStruct((2, length, inner), BF16),
        compiler_params=params(2, 12),
        name="finish",
    )(y, bc, entering, aux, gate_in, gain)


def project_out_kernel(
    count, normed_ref, w_ref, out_ref, held, sending, landed, send_sems, recv_sems
):
    me = lax.axis_index("head")
    bits = count.bit_length() - 1
    inner, depth = w_ref.shape
    half = depth // count // 2
    tile = min(half, COLS)
    orders = (list(range(bits)), list(range(bits))[::-1])

    barrier = pltpu.get_barrier_semaphore()
    for bit in range(bits):
        pl.semaphore_signal(
            barrier, inc=1, device_id={"head": me ^ (1 << bit)},
            device_id_type=pl.DeviceIdType.MESH,
        )
    pl.semaphore_wait(barrier, bits)

    def phase_of(side, mask):
        return next(p for p, bit in enumerate(orders[side]) if mask >> bit & 1)

    def copy_of(side, mask):
        slot = side * (count - 1) + mask - 1
        partner = me ^ (1 << orders[side][phase_of(side, mask)])
        return pltpu.make_async_remote_copy(
            src_ref=sending.at[slot],
            dst_ref=landed.at[slot],
            send_sem=send_sems.at[slot],
            recv_sem=recv_sems.at[slot],
            device_id={"head": partner},
            device_id_type=pl.DeviceIdType.MESH,
        )

    def partial(side, mask, store):
        first = (me ^ mask) * (2 * half) + side * half
        flip = anti_identity(tile)

        def one(j, carry):
            at = pl.multiple_of(first + j * tile, tile)
            mirrored = pl.multiple_of(depth - tile - at, tile)
            flipped = matmul(w_ref[:, pl.ds(mirrored, tile)], flip).astype(BF16)
            value = matmul(normed_ref[0], w_ref[:, pl.ds(at, tile)]) + matmul(
                normed_ref[1], flipped
            )
            store(pl.ds(pl.multiple_of(j * tile, tile), tile), value)
            return carry

        lax.fori_loop(0, half // tile, one, 0)

    def into_sending(slot):
        def store(columns, value):
            sending[slot, :, columns] = value.astype(BF16)

        return store

    def into_held(slot):
        def store(columns, value):
            held[slot, :, columns] = value

        return store

    pieces = sorted(
        ((phase_of(side, mask), -bin(mask).count("1"), mask, side)
         for side in range(2) for mask in range(1, count)),
        key=lambda piece: piece[:2],
    )
    later = [(side, mask) for phase, _, mask, side in pieces if phase > 0] + [(0, 0), (1, 0)]
    for phase, _, mask, side in pieces:
        if phase == 0:
            partial(side, mask, into_sending(side * (count - 1) + mask - 1))
            copy_of(side, mask).start()
    for place, (side, mask) in enumerate(later):
        partial(side, mask, into_held(place))
    for place, (side, mask) in enumerate(later):
        total = held[place]
        for q in range(phase_of(side, mask) if mask else bits):
            source = mask | 1 << orders[side][q]
            copy_of(side, source).wait_recv()
            total = total + landed[side * (count - 1) + source - 1].astype(F32)
        if mask:
            sending[side * (count - 1) + mask - 1] = total.astype(BF16)
            copy_of(side, mask).start()
        else:
            out_ref[:, side * half : (side + 1) * half] = total.astype(BF16)
    for _, _, mask, side in pieces:
        copy_of(side, mask).wait_send()


def project_out(normed, w_out):
    _, length, inner = normed.shape
    depth = w_out.shape[1]
    count = lax.axis_size("head")
    half = depth // count // 2
    slots = 2 * (count - 1)
    return pl.pallas_call(
        functools.partial(project_out_kernel, count),
        in_specs=[pl.BlockSpec(memory_space=pltpu.VMEM)] * 2,
        out_specs=pl.BlockSpec(memory_space=pltpu.VMEM),
        out_shape=jax.ShapeDtypeStruct((length, depth // count), BF16),
        scratch_shapes=[
            pltpu.VMEM((count, length, half), F32),
            pltpu.VMEM((slots, length, half), BF16),
            pltpu.VMEM((slots, length, half), BF16),
            pltpu.SemaphoreType.DMA((slots,)),
            pltpu.SemaphoreType.DMA((slots,)),
        ],
        compiler_params=pltpu.CompilerParams(
            vmem_limit_bytes=28 * MIB, collective_id=0, has_side_effects=True
        ),
        name="project_out",
    )(normed, w_out)


def shards(
    hidden, base_ids, norm_gain, w_gate, w_value, w_bc, w_step, conv_value, conv_bc,
    step_bias, decay_rate, skip_gain, out_gain, w_out,
):
    keep = (base_ids != 4).astype(F32)[:, None]
    length, depth = hidden.shape
    inner = w_gate.shape[1]
    heads = w_step.shape[1]
    width = inner // heads
    chunks = inner // COLS
    per = COLS // width
    scaled, squares = prepare(hidden, norm_gain)
    inv_rms = lax.rsqrt(jnp.sum(squares, axis=-1) / depth + EPSILON)[:, None]

    def project(weight):
        return (
            jnp.einsum("btd,dk->btk", scaled, weight, preferred_element_type=F32) * inv_rms
        )

    bc_in = project(w_bc)
    step_in = project(w_step)
    value_in = project(w_value)
    size = lax.axis_size("ctx")
    up = [(i, i + 1) for i in range(size - 1)]
    down = [(i + 1, i) for i in range(size - 1)]
    tail = jnp.concatenate([value_in[:, length - HALO :], bc_in[:, length - HALO :]], axis=-1)
    head = jnp.concatenate([value_in[:, :HALO], bc_in[:, :HALO]], axis=-1)
    before = lax.ppermute(tail, "ctx", up)
    after = lax.ppermute(head, "ctx", down)
    gate_in = project(w_gate)

    steps = jax.nn.softplus(step_in + step_bias)
    log_decay = -decay_rate * steps
    lower = jnp.tril(jnp.ones((length, length), F32))
    triangles = jnp.stack([lower, lower.T])
    cum = jnp.einsum("dts,bsh->bdth", triangles, log_decay, precision=PRECISE)
    log_total = cum[:, 0, -1]
    packed = jnp.concatenate([cum, steps[:, None]], axis=1)
    packed = packed.reshape(2, 3, length, chunks, per)
    aux = packed.transpose(0, 3, 2, 1, 4).reshape(2, chunks, length, 3 * per)
    lines = (cum - jnp.log(steps)[:, None]).reshape(2, 2, length, chunks, per)
    rows = lines.transpose(0, 3, 1, 4, 2).reshape(2, chunks, 2 * per, length)

    x, bc, bt, local = mix(value_in, bc_in, before, after, conv_value, conv_bc, aux, keep)
    total = jnp.broadcast_to(jnp.repeat(log_total, width, axis=-1)[:, None], (2, 8, inner))
    y, entering = scan_local(
        x, bc, bt, aux, rows, jnp.repeat(skip_gain, width)[None], local, total
    )
    normed = finish(y, bc, entering, aux, gate_in, out_gain[None])
    return project_out(normed, w_out)


def solution(mesh):
    return jax.shard_map(
        shards,
        mesh=mesh,
        in_specs=(
            P("ctx", None),
            P("ctx"),
            P(),
            P(None, "head"),
            P(None, "head"),
            P(),
            P(None, "head"),
            P(None, "head"),
            P(),
            P("head"),
            P("head"),
            P("head"),
            P("head"),
            P("head", None),
        ),
        out_specs=P("ctx", "head"),
        check_vma=False,
    )
```

```python
import functools

import jax
import jax.numpy as jnp
from jax import lax
from jax.experimental import pallas as pl
from jax.experimental.pallas import tpu as pltpu
from jax.sharding import PartitionSpec as P

EPSILON = 1e-05
PRECISE = lax.Precision.HIGHEST
F32 = jnp.float32
BF16 = jnp.bfloat16
COLS = 256
ROWS = 128
HALO = 8
MIB = 1024 * 1024


def params(dims, mib):
    return pltpu.CompilerParams(
        vmem_limit_bytes=mib * MIB, dimension_semantics=("arbitrary",) * dims
    )


def anti_identity(size):
    row = lax.broadcasted_iota(jnp.int32, (size, size), 0)
    col = lax.broadcasted_iota(jnp.int32, (size, size), 1)
    return (row + col == size - 1).astype(F32).astype(BF16)


def matmul(a, b):
    return jnp.dot(a, b, preferred_element_type=F32)


def spread(per_head, width):
    heads = per_head.shape[1]
    high = per_head.astype(BF16)
    low = (per_head - high.astype(F32)).astype(BF16)
    row = lax.broadcasted_iota(jnp.int32, (2 * heads, heads * width), 0)
    col = lax.broadcasted_iota(jnp.int32, (2 * heads, heads * width), 1)
    row = jnp.where(row < heads, row, row - heads)
    pick = ((col >= row * width) & (col < (row + 1) * width)).astype(F32).astype(BF16)
    return matmul(jnp.concatenate([high, low], axis=1), pick)


def silu(x):
    half = 0.5 * x
    return half + half * jnp.tanh(half)


def prepare_kernel(
    depth, own_ref, mirror_ref, gain_ref, w_bc_ref, w_step_ref,
    scaled_ref, bc_ref, step_ref, inv_ref, squares_ref,
):
    flip = anti_identity(COLS)
    parts = own_ref.shape[1] // COLS
    squares = None
    for q in range(parts):
        at = slice(q * COLS, (q + 1) * COLS)
        opposite = slice((parts - 1 - q) * COLS, (parts - q) * COLS)
        own = own_ref[:, at].astype(F32)
        gain = gain_ref[:, at]
        scaled_ref[0, :, at] = (own * gain).astype(BF16)
        scaled_ref[1, :, at] = (matmul(mirror_ref[:, opposite], flip) * gain).astype(BF16)
        square = own * own
        square = square[:, :128] + square[:, 128:]
        squares = square if squares is None else squares + square

    @pl.when(pl.program_id(0) == 0)
    def _():
        squares_ref[...] = squares
        for b in range(2):
            bc_ref[b] = matmul(scaled_ref[b], w_bc_ref[...])
            step_ref[b] = matmul(scaled_ref[b], w_step_ref[...])

    @pl.when(pl.program_id(0) > 0)
    def _():
        squares_ref[...] += squares
        for b in range(2):
            bc_ref[b] += matmul(scaled_ref[b], w_bc_ref[...])
            step_ref[b] += matmul(scaled_ref[b], w_step_ref[...])

    @pl.when(pl.program_id(0) == pl.num_programs(0) - 1)
    def _():
        total = jnp.sum(squares_ref[...], axis=1, keepdims=True)
        inv = lax.rsqrt(total * (1.0 / depth) + EPSILON)
        inv_ref[...] = inv
        for b in range(2):
            bc_ref[b] = bc_ref[b] * inv
            step_ref[b] = step_ref[b] * inv


def prepare(hidden, gain, w_bc, w_step):
    length, depth = hidden.shape
    pair, heads = w_bc.shape[1], w_step.shape[1]
    span = 4 * COLS
    count = depth // span
    return pl.pallas_call(
        functools.partial(prepare_kernel, depth),
        grid=(count,),
        in_specs=[
            pl.BlockSpec((length, span), lambda j: (0, j)),
            pl.BlockSpec((length, span), lambda j: (0, count - 1 - j)),
            pl.BlockSpec((1, span), lambda j: (0, j)),
            pl.BlockSpec((span, pair), lambda j: (j, 0)),
            pl.BlockSpec((span, heads), lambda j: (j, 0)),
        ],
        out_specs=[
            pl.BlockSpec((2, length, span), lambda j: (0, 0, j)),
            pl.BlockSpec((2, length, pair), lambda j: (0, 0, 0)),
            pl.BlockSpec((2, length, heads), lambda j: (0, 0, 0)),
            pl.BlockSpec((length, 1), lambda j: (0, 0)),
        ],
        out_shape=[
            jax.ShapeDtypeStruct((2, length, depth), BF16),
            jax.ShapeDtypeStruct((2, length, pair), F32),
            jax.ShapeDtypeStruct((2, length, heads), F32),
            jax.ShapeDtypeStruct((length, 1), F32),
        ],
        scratch_shapes=[pltpu.VMEM((length, 128), F32)],
        compiler_params=params(1, 20),
        name="prepare",
    )(hidden, hidden, gain[None], w_bc, w_step)


def convolve(out, ext, main_ref, before_ref, after_ref, taps_ref):
    length = main_ref.shape[1]
    ext[0:HALO] = before_ref[0]
    ext[HALO : HALO + length] = main_ref[0]
    ext[HALO + length :] = after_ref[0]
    taps = [taps_ref[k : k + 1, :] for k in range(4)]
    step = 64
    for start in range(0, length, step):
        rows = [ext[start + HALO - 3 + k : start + HALO - 3 + k + step] for k in range(7)]
        forward = taps[0] * rows[0]
        backward = taps[0] * rows[6]
        for k in range(1, 4):
            forward = forward + taps[k] * rows[k]
            backward = backward + taps[k] * rows[6 - k]
        out(start, step, silu(forward), silu(backward))


def mix_kernel(
    v_ref, bc_ref, before_v, before_bc, after_v, after_bc, taps_v, taps_bc, aux_ref, keep_ref,
    x_ref, bco_ref, bt_ref, s_ref, ext,
):
    c = pl.program_id(1)
    length = v_ref.shape[1]

    @pl.when(c == 0)
    def _():
        def out(start, step, forward, backward):
            bco_ref[0, 0, start : start + step] = forward.astype(BF16)
            bco_ref[0, 1, start : start + step] = backward.astype(BF16)

        convolve(out, ext, bc_ref, before_bc, after_bc, taps_bc)
        state = bt_ref.shape[2]
        for d in range(2):
            bt_ref[0, d] = bco_ref[0, d, :, :state].astype(F32).T.astype(BF16)

    @pl.when(c > 0)
    def _():
        def out(start, step, forward, backward):
            keep = keep_ref[start : start + step]
            x_ref[0, 0, start : start + step] = (forward * keep).astype(BF16)
            x_ref[0, 1, start : start + step] = (backward * keep).astype(BF16)

        convolve(out, ext, v_ref, before_v, after_v, taps_v)
        heads = aux_ref.shape[3] // 3
        aux = aux_ref[0, 0]
        steps = aux[:, 2 * heads :]
        for d in range(2):
            cum = aux[:, d * heads : (d + 1) * heads]
            total = cum[length - 1 :] if d == 0 else cum[:1]
            weight = spread(jnp.exp(total - cum) * steps, COLS // heads)
            s_ref[0, d] = matmul(bt_ref[0, d], (x_ref[0, d].astype(F32) * weight).astype(BF16))


def mix(value_in, bc_in, before, after, conv_value, conv_bc, aux, keep):
    _, length, inner = value_in.shape
    pair = bc_in.shape[2]
    state = pair // 2
    chunks = inner // COLS

    def at(c):
        return jnp.maximum(c - 1, 0)

    return pl.pallas_call(
        mix_kernel,
        grid=(2, chunks + 1),
        in_specs=[
            pl.BlockSpec((1, length, COLS), lambda b, c: (b, 0, at(c))),
            pl.BlockSpec((1, length, pair), lambda b, c: (b, 0, 0)),
            pl.BlockSpec((1, HALO, COLS), lambda b, c: (b, 0, at(c))),
            pl.BlockSpec((1, HALO, pair), lambda b, c: (b, 0, inner // pair)),
            pl.BlockSpec((1, HALO, COLS), lambda b, c: (b, 0, at(c))),
            pl.BlockSpec((1, HALO, pair), lambda b, c: (b, 0, inner // pair)),
            pl.BlockSpec((4, COLS), lambda b, c: (0, at(c))),
            pl.BlockSpec((4, pair), lambda b, c: (0, 0)),
            pl.BlockSpec((1, 1) + aux.shape[2:], lambda b, c: (b, at(c), 0, 0)),
            pl.BlockSpec((length, 1), lambda b, c: (0, 0)),
        ],
        out_specs=[
            pl.BlockSpec((1, 2, length, COLS), lambda b, c: (b, 0, 0, at(c))),
            pl.BlockSpec((1, 2, length, pair), lambda b, c: (b, 0, 0, 0)),
            pl.BlockSpec((1, 2, state, length), lambda b, c: (b, 0, 0, 0)),
            pl.BlockSpec((1, 2, state, COLS), lambda b, c: (b, 0, 0, at(c))),
        ],
        out_shape=[
            jax.ShapeDtypeStruct((2, 2, length, inner), BF16),
            jax.ShapeDtypeStruct((2, 2, length, pair), BF16),
            jax.ShapeDtypeStruct((2, 2, state, length), BF16),
            jax.ShapeDtypeStruct((2, 2, state, inner), F32),
        ],
        scratch_shapes=[pltpu.VMEM((length + 2 * HALO, COLS), F32)],
        compiler_params=params(2, 16),
        cost_estimate=pl.CostEstimate(
            flops=2 * 4 * length * state * inner,
            bytes_accessed=14 * 2 * length * inner,
            transcendentals=4 * length * inner,
        ),
        name="mix",
    )(value_in, bc_in, before, before, after, after, conv_value, conv_bc, aux, keep)


def chain(size, last, local_ref, total_ref, ent_ref, swapped, decay_other, chip, kept,
          hop_out, hop_in, crossed, send_sems, recv_sems):
    me = lax.axis_index("ctx")
    odd = lax.rem(me, 2)
    ahead = me + 4 * odd - 2
    behind = me - 4 * odd + 2
    has_ahead = (ahead >= 0) & (ahead < size)
    has_behind = (behind >= 0) & (behind < size)
    partner = me + 1 - 2 * odd
    place = me // 2 * (2 * odd - 1) + (1 - odd) * (size // 2 - 1)

    def remote(source, target, index, device):
        return pltpu.make_async_remote_copy(
            src_ref=source,
            dst_ref=target,
            send_sem=send_sems.at[index],
            recv_sem=recv_sems.at[index],
            device_id={"ctx": device},
            device_id_type=pl.DeviceIdType.MESH,
        )

    swap_copy = remote(kept, swapped, 0, partner)
    decay_copy = remote(total_ref, decay_other, 1, partner)
    cross_copies = [remote(kept.at[b], crossed.at[b], 2 + b, partner) for b in range(2)]
    hop_copies = [remote(hop_out.at[b], hop_in.at[b], 4 + b, ahead) for b in range(2)]

    def greet():
        barrier = pltpu.get_barrier_semaphore()

        def signal(device):
            pl.semaphore_signal(
                barrier, inc=1, device_id={"ctx": device}, device_id_type=pl.DeviceIdType.MESH
            )

        signal(partner)
        pl.when(has_ahead)(lambda: signal(ahead))
        pl.when(has_behind)(lambda: signal(behind))
        pl.semaphore_wait(
            barrier, 1 + has_ahead.astype(jnp.int32) + has_behind.astype(jnp.int32)
        )

    def first():
        greet()
        for b in range(2):
            kept[b] = jnp.where(odd == 1, local_ref[b, 1], local_ref[b, 0]).astype(BF16)
        swap_copy.start()
        decay_copy.start()

    def second():
        swap_copy.wait()
        decay_copy.wait()
        for b in range(2):
            mine = jnp.where(odd == 1, local_ref[b, 0], local_ref[b, 1])
            decay = jnp.exp(total_ref[b, :1])
            chip[b] = decay * swapped[b].astype(F32) + mine

    def link(b):
        def stage():
            pl.when(has_behind)(lambda: hop_copies[b].wait_recv())
            decay = jnp.exp(total_ref[b, :1] + decay_other[b, :1])
            entering = jnp.where(has_behind, hop_in[b].astype(F32), 0.0)
            hop_out[b] = (chip[b] + decay * entering).astype(BF16)
            pl.when(has_ahead)(lambda: hop_copies[b].start())
            kept[b] = entering.astype(BF16)
            cross_copies[b].start()

        return stage

    def end():
        for b in range(2):
            cross_copies[b].wait()
            own = jnp.exp(decay_other[b, :1]) * kept[b].astype(F32) + swapped[b].astype(F32)
            other = crossed[b].astype(F32)
            ent_ref[b, 0] = jnp.where(odd == 1, own, other).astype(BF16)
            ent_ref[b, 1] = jnp.where(odd == 1, other, own).astype(BF16)
            pl.when(has_ahead)(lambda b=b: hop_copies[b].wait_send())

    stages = [(0, first), (1, second)]
    stages += [(jnp.minimum(place + b + 1, last), link(b)) for b in range(2)]
    return stages, end


def scan_kernel(size, x_ref, bc_ref, bt_ref, aux_ref, row_ref, skip_ref, local_ref, total_ref,
                y_ref, ent_ref, *scratch):
    step = pl.program_id(0) * pl.num_programs(1) + pl.program_id(1)
    last_step = 2 * (local_ref.shape[3] // COLS) - 1
    stages, end = chain(size, last_step, local_ref, total_ref, ent_ref, *scratch)
    for at, stage in stages:
        pl.when(step == at)(stage)
    length = x_ref.shape[2]
    state = bt_ref.shape[2]
    heads = aux_ref.shape[3] // 3
    width = COLS // heads
    row = lax.broadcasted_iota(jnp.int32, (ROWS, ROWS), 0)
    col = lax.broadcasted_iota(jnp.int32, (ROWS, ROWS), 1)
    on_left = lax.broadcasted_iota(jnp.int32, (1, 2 * width), 1) < width
    left = on_left.astype(F32).astype(BF16)
    right = (1.0 - on_left.astype(F32)).astype(BF16)
    blocks = length // ROWS

    def diagonal(pair):
        return jnp.concatenate([pair * left, pair * right], axis=0)

    for d in range(2):
        carried = [None] * (heads // 2)
        reach = (row >= col) if d == 0 else (row <= col)
        order = range(blocks) if d == 0 else range(blocks - 1, -1, -1)
        for lap, i in enumerate(order):
            own = slice(i * ROWS, (i + 1) * ROWS)
            cum = aux_ref[0, 0, own, d * heads : (d + 1) * heads]
            lines = row_ref[0, 0, d * heads : (d + 1) * heads, own]
            c_rows = bc_ref[0, d, own, state:]
            c_wide = c_rows.astype(F32)
            b_wide = bt_ref[0, d, :, own].astype(F32)
            scores = lax.dot_general(
                c_rows, bc_ref[0, d, own, :state], (((1,), (1,)), ((), ())),
                preferred_element_type=F32,
            )
            final = cum[ROWS - 1 :] if d == 0 else cum[:1]
            if lap > 0:
                entry = (i * ROWS - 1) if d == 0 else (i + 1) * ROWS
                base = aux_ref[0, 0, entry : entry + 1, d * heads : (d + 1) * heads]
            for p in range(heads // 2):
                weights, tails, entries, decays = [], [], [], []
                for h in (2 * p, 2 * p + 1):
                    tall = jnp.broadcast_to(cum[:, h : h + 1], (ROWS, ROWS))
                    line = lines[h : h + 1]
                    gap = jnp.where(reach, tall - line, -jnp.inf)
                    weights.append((jnp.exp(gap) * scores).astype(BF16))
                    if lap < blocks - 1:
                        tails.append((b_wide * jnp.exp(final[:, h : h + 1] - line)).astype(BF16))
                    if lap > 0:
                        start = base[:, h : h + 1]
                        entries.append((c_wide * jnp.exp(tall - start)).astype(BF16))
                        decays.append(jnp.exp(final[:, h : h + 1] - start))
                at = slice(2 * p * width, 2 * (p + 1) * width)
                x = x_ref[0, d, own, at]
                lhs = jnp.concatenate(weights, axis=1)
                if tails:
                    lhs = jnp.concatenate([lhs, jnp.concatenate(tails, axis=1)], axis=0)
                result = matmul(lhs, diagonal(x))
                local = result[:ROWS] + skip_ref[:, at] * x.astype(F32)
                if entries:
                    local = local + matmul(
                        jnp.concatenate(entries, axis=1), diagonal(carried[p].astype(BF16))
                    )
                if tails:
                    fresh = result[ROWS:]
                    if entries:
                        fresh = jnp.where(on_left, decays[0], decays[1]) * carried[p] + fresh
                    carried[p] = fresh
                if d == 0:
                    y_ref[0, own, at] = local
                else:
                    y_ref[0, own, at] += local
    pl.when(step == last_step)(end)


def scan_local(x, bc, bt, aux, rows, skip, local, total):
    size = lax.axis_size("ctx")
    wide = local.shape[2:]
    _, _, length, inner = x.shape
    pair = bc.shape[3]
    state = pair // 2
    chunks = inner // COLS
    return pl.pallas_call(
        functools.partial(scan_kernel, size),
        grid=(2, chunks),
        in_specs=[
            pl.BlockSpec((1, 2, length, COLS), lambda b, c: (b, 0, 0, c)),
            pl.BlockSpec((1, 2, length, pair), lambda b, c: (b, 0, 0, 0)),
            pl.BlockSpec((1, 2, state, length), lambda b, c: (b, 0, 0, 0)),
            pl.BlockSpec((1, 1) + aux.shape[2:], lambda b, c: (b, c, 0, 0)),
            pl.BlockSpec((1, 1) + rows.shape[2:], lambda b, c: (b, c, 0, 0)),
            pl.BlockSpec((1, COLS), lambda b, c: (0, c)),
            pl.BlockSpec(local.shape, lambda b, c: (0, 0, 0, 0)),
            pl.BlockSpec(total.shape, lambda b, c: (0, 0, 0)),
        ],
        out_specs=[
            pl.BlockSpec((1, length, COLS), lambda b, c: (b, 0, c)),
            pl.BlockSpec(local.shape, lambda b, c: (0, 0, 0, 0)),
        ],
        out_shape=[
            jax.ShapeDtypeStruct((2, length, inner), F32),
            jax.ShapeDtypeStruct(local.shape, BF16),
        ],
        scratch_shapes=[
            pltpu.VMEM((2,) + wide, BF16),
            pltpu.VMEM(total.shape, F32),
            pltpu.VMEM((2,) + wide, F32),
            pltpu.VMEM((2,) + wide, BF16),
            pltpu.VMEM((2,) + wide, BF16),
            pltpu.VMEM((2,) + wide, BF16),
            pltpu.VMEM((2,) + wide, BF16),
            pltpu.SemaphoreType.DMA((6,)),
            pltpu.SemaphoreType.DMA((6,)),
        ],
        compiler_params=pltpu.CompilerParams(
            vmem_limit_bytes=28 * MIB,
            dimension_semantics=("arbitrary",) * 2,
            collective_id=1,
            has_side_effects=True,
        ),
        cost_estimate=pl.CostEstimate(
            flops=2 * 64 * length * ROWS * inner,
            bytes_accessed=20 * length * inner,
            transcendentals=0,
        ),
        name="scan_local",
    )(x, bc, bt, aux, rows, skip, local, total)


def finish_kernel(y_ref, bc_ref, s_ref, aux_ref, gate_ref, gain_ref, out_ref):
    state = s_ref.shape[2]
    heads = aux_ref.shape[3] // 3
    width = COLS // heads
    row = lax.broadcasted_iota(jnp.int32, (COLS, COLS), 0)
    col = lax.broadcasted_iota(jnp.int32, (COLS, COLS), 1)
    same = None
    for h in range(heads):
        low, high = h * width, (h + 1) * width
        square = (row >= low) & (row < high) & (col >= low) & (col < high)
        same = square if same is None else same | square
    same = same.astype(F32).astype(BF16)
    length = y_ref.shape[1]
    for start in range(0, length, 2 * ROWS):
        own = slice(start, start + 2 * ROWS)
        aux = aux_ref[0, 0, own]
        y = y_ref[0, own]
        for d in range(2):
            grown = spread(jnp.exp(aux[:, d * heads : (d + 1) * heads]), width)
            y = y + grown * matmul(bc_ref[0, d, own, state:], s_ref[0, d])
        gated = y * silu(gate_ref[0, own])
        mean = matmul((gated * gated).astype(BF16), same) * (1.0 / width)
        out_ref[0, own] = (gated * lax.rsqrt(mean + EPSILON) * gain_ref[...]).astype(BF16)


def finish(y, bc, entering, aux, gate_in, gain):
    _, length, inner = y.shape
    pair = bc.shape[3]
    chunks = inner // COLS
    return pl.pallas_call(
        finish_kernel,
        grid=(2, chunks),
        in_specs=[
            pl.BlockSpec((1, length, COLS), lambda b, c: (b, 0, c)),
            pl.BlockSpec((1, 2, length, pair), lambda b, c: (b, 0, 0, 0)),
            pl.BlockSpec((1, 2, pair // 2, COLS), lambda b, c: (b, 0, 0, c)),
            pl.BlockSpec((1, 1) + aux.shape[2:], lambda b, c: (b, c, 0, 0)),
            pl.BlockSpec((1, length, COLS), lambda b, c: (b, 0, c)),
            pl.BlockSpec((1, COLS), lambda b, c: (0, c)),
        ],
        out_specs=pl.BlockSpec((1, length, COLS), lambda b, c: (b, 0, c)),
        out_shape=jax.ShapeDtypeStruct((2, length, inner), BF16),
        compiler_params=params(2, 12),
        name="finish",
    )(y, bc, entering, aux, gate_in, gain)


def project_out_kernel(
    count, normed_ref, w_ref, out_ref, held, sending, landed, send_sems, recv_sems
):
    me = lax.axis_index("head")
    bits = count.bit_length() - 1
    inner, depth = w_ref.shape
    half = depth // count // 2
    tile = min(half, COLS)
    orders = (list(range(bits)), list(range(bits))[::-1])

    barrier = pltpu.get_barrier_semaphore()
    for bit in range(bits):
        pl.semaphore_signal(
            barrier, inc=1, device_id={"head": me ^ (1 << bit)},
            device_id_type=pl.DeviceIdType.MESH,
        )
    pl.semaphore_wait(barrier, bits)

    def phase_of(side, mask):
        return next(p for p, bit in enumerate(orders[side]) if mask >> bit & 1)

    def copy_of(side, mask):
        slot = side * (count - 1) + mask - 1
        partner = me ^ (1 << orders[side][phase_of(side, mask)])
        return pltpu.make_async_remote_copy(
            src_ref=sending.at[slot],
            dst_ref=landed.at[slot],
            send_sem=send_sems.at[slot],
            recv_sem=recv_sems.at[slot],
            device_id={"head": partner},
            device_id_type=pl.DeviceIdType.MESH,
        )

    def partial(side, mask, store):
        first = (me ^ mask) * (2 * half) + side * half
        flip = anti_identity(tile)

        def one(j, carry):
            at = pl.multiple_of(first + j * tile, tile)
            mirrored = pl.multiple_of(depth - tile - at, tile)
            flipped = matmul(w_ref[:, pl.ds(mirrored, tile)], flip).astype(BF16)
            value = matmul(normed_ref[0], w_ref[:, pl.ds(at, tile)]) + matmul(
                normed_ref[1], flipped
            )
            store(pl.ds(pl.multiple_of(j * tile, tile), tile), value)
            return carry

        lax.fori_loop(0, half // tile, one, 0)

    def into_sending(slot):
        def store(columns, value):
            sending[slot, :, columns] = value.astype(BF16)

        return store

    def into_held(slot):
        def store(columns, value):
            held[slot, :, columns] = value

        return store

    pieces = sorted(
        ((phase_of(side, mask), -bin(mask).count("1"), mask, side)
         for side in range(2) for mask in range(1, count)),
        key=lambda piece: piece[:2],
    )
    later = [(side, mask) for phase, _, mask, side in pieces if phase > 0] + [(0, 0), (1, 0)]
    for phase, _, mask, side in pieces:
        if phase == 0:
            partial(side, mask, into_sending(side * (count - 1) + mask - 1))
            copy_of(side, mask).start()
    for place, (side, mask) in enumerate(later):
        partial(side, mask, into_held(place))
    for place, (side, mask) in enumerate(later):
        total = held[place]
        for q in range(phase_of(side, mask) if mask else bits):
            source = mask | 1 << orders[side][q]
            copy_of(side, source).wait_recv()
            total = total + landed[side * (count - 1) + source - 1].astype(F32)
        if mask:
            sending[side * (count - 1) + mask - 1] = total.astype(BF16)
            copy_of(side, mask).start()
        else:
            out_ref[:, side * half : (side + 1) * half] = total.astype(BF16)
    for _, _, mask, side in pieces:
        copy_of(side, mask).wait_send()


def project_out(normed, w_out):
    _, length, inner = normed.shape
    depth = w_out.shape[1]
    count = lax.axis_size("head")
    half = depth // count // 2
    slots = 2 * (count - 1)
    return pl.pallas_call(
        functools.partial(project_out_kernel, count),
        in_specs=[pl.BlockSpec(memory_space=pltpu.VMEM)] * 2,
        out_specs=pl.BlockSpec(memory_space=pltpu.VMEM),
        out_shape=jax.ShapeDtypeStruct((length, depth // count), BF16),
        scratch_shapes=[
            pltpu.VMEM((count, length, half), F32),
            pltpu.VMEM((slots, length, half), BF16),
            pltpu.VMEM((slots, length, half), BF16),
            pltpu.SemaphoreType.DMA((slots,)),
            pltpu.SemaphoreType.DMA((slots,)),
        ],
        compiler_params=pltpu.CompilerParams(
            vmem_limit_bytes=28 * MIB, collective_id=0, has_side_effects=True
        ),
        name="project_out",
    )(normed, w_out)


def shards(
    hidden, base_ids, norm_gain, w_gate, w_value, w_bc, w_step, conv_value, conv_bc,
    step_bias, decay_rate, skip_gain, out_gain, w_out,
):
    keep = (base_ids != 4).astype(F32)[:, None]
    length = hidden.shape[0]
    inner = w_gate.shape[1]
    heads = w_step.shape[1]
    width = inner // heads
    chunks = inner // COLS
    per = COLS // width
    scaled, bc_in, step_in, inv_rms = prepare(hidden, norm_gain, w_bc, w_step)

    def project(weight):
        return (
            jnp.einsum("btd,dk->btk", scaled, weight, preferred_element_type=F32) * inv_rms
        )

    value_in = project(w_value)
    size = lax.axis_size("ctx")
    up = [(i, i + 1) for i in range(size - 1)]
    down = [(i + 1, i) for i in range(size - 1)]
    tail = jnp.concatenate([value_in[:, length - HALO :], bc_in[:, length - HALO :]], axis=-1)
    head = jnp.concatenate([value_in[:, :HALO], bc_in[:, :HALO]], axis=-1)
    before = lax.ppermute(tail, "ctx", up)
    after = lax.ppermute(head, "ctx", down)
    gate_in = project(w_gate)

    steps = jax.nn.softplus(step_in + step_bias)
    log_decay = -decay_rate * steps
    lower = jnp.tril(jnp.ones((length, length), F32))
    triangles = jnp.stack([lower, lower.T])
    cum = jnp.einsum("dts,bsh->bdth", triangles, log_decay, precision=PRECISE)
    log_total = cum[:, 0, -1]
    packed = jnp.concatenate([cum, steps[:, None]], axis=1)
    packed = packed.reshape(2, 3, length, chunks, per)
    aux = packed.transpose(0, 3, 2, 1, 4).reshape(2, chunks, length, 3 * per)
    lines = (cum - jnp.log(steps)[:, None]).reshape(2, 2, length, chunks, per)
    rows = lines.transpose(0, 3, 1, 4, 2).reshape(2, chunks, 2 * per, length)

    x, bc, bt, local = mix(value_in, bc_in, before, after, conv_value, conv_bc, aux, keep)
    total = jnp.broadcast_to(jnp.repeat(log_total, width, axis=-1)[:, None], (2, 8, inner))
    y, entering = scan_local(
        x, bc, bt, aux, rows, jnp.repeat(skip_gain, width)[None], local, total
    )
    normed = finish(y, bc, entering, aux, gate_in, out_gain[None])
    return project_out(normed, w_out)


def solution(mesh):
    return jax.shard_map(
        shards,
        mesh=mesh,
        in_specs=(
            P("ctx", None),
            P("ctx"),
            P(),
            P(None, "head"),
            P(None, "head"),
            P(),
            P(None, "head"),
            P(None, "head"),
            P(),
            P("head"),
            P("head"),
            P("head"),
            P("head"),
            P("head", None),
        ),
        out_specs=P("ctx", "head"),
        check_vma=False,
    )
```
